32 devices in a mesh: groups: 2 (over x), pool: 8 (over z, y), tensor: 2 (over core).
Axes of the slice: x: 2, y: 2, z: 4, core: 2. Of those that a mesh axis runs over, the one named last changes fastest.
Arguments:
- hidden: bfloat16 [384, 8192], P(('groups', 'pool'), 'tensor'), parts along dimension 0, may hold values from -6 to 6
- adapter_ids: int32 [384, 1], P(('groups', 'pool')), parts along dimension 0, may hold values from 0 to 7; in each aligned block of 24 rows (0 to 23, 24 to 47, ...) at most 6 rows name the same one
- page_table: int32 [8], replicated, may hold values from 0 to 7, each once
- gate_weight: bfloat16 [8192, 14336], P('tensor', 'pool'), may hold values from -0.0625 to 0.0625
- up_weight: bfloat16 [8192, 14336], P('tensor', 'pool'), may hold values from -0.0625 to 0.0625
- shrink: bfloat16 [8, 8192, 64], P('pool', 'tensor'), may hold values from -0.0625 to 0.0625
- gate_expander_matrices: bfloat16 [8, 32, 14336], P(None, None, 'pool'), may hold values from -1 to 1
- up_expander_matrices: bfloat16 [8, 32, 14336], P(None, None, 'pool'), may hold values from -1 to 1
Outputs:
- activated: bfloat16 [384, 14336], P(('groups', 'pool')), parts along dimension 0
The draws below stay inside these ranges and needn't reach their ends.
There are 2 independent parts, one for each index of `groups`. The reference program is written for one: setup_inputs(seed, part) draws one part's arguments, and reference() takes and returns one part's arrays. A program takes and returns all parts, laid end to end along the dimension named above; an argument that names none is the same for every part. Nothing has to cross between parts.
Inputs may be any that keep to these rules, and one draw needn't show every extreme that they name: `adapter_ids`: in the 24 rows of one pool device no adapter is named by more than 6 rows, and in some device's rows one adapter is named by exactly 6; every adapter is named by some row. `page_table`: each slot is held by exactly one adapter.
All inputs are finite; a program needn't handle non-finite values.
Results may differ from the reference program's by a relative error of at most 0.0037.
Values may be sent and summed in bfloat16 or wider, within the bound.
A program may use at most 128 MiB of HBM per device.

```python
import math
import jax
import jax.numpy as jnp
import numpy as np

D = 8192
FF_WIN = 14336
R = 32
ROWS_DEV = 24
ADAPTERS = 8
MOST = 6
ROWS = 192


def levels(own_key, dims, pieces, low, largest):
    def one(dim, blocks):
        draws = jax.random.uniform(jax.random.fold_in(jax.random.fold_in(own_key, 6), dim), (blocks,), jnp.float32, low / len(pieces), largest / len(pieces))
        return jnp.repeat(jnp.exp(draws), dims[dim] // blocks).reshape((-1,) + (1,) * (len(dims) - dim - 1))

    loudness = one(*pieces[0])
    for cut in pieces[1:]:
        loudness = loudness * one(*cut)
    return loudness


def shared_out(own_key, own, number, rows, amount, top, bound, slope):
    order = jax.random.permutation(own_key, amount)
    heavy_load, usual = load_shares(amount, rows * top, bound, slope, True), load_shares(amount, rows * top, bound, slope, False)
    places = jnp.arange(amount)

    def named(tallies, rotation):
        used = int((tallies > 0).sum())
        fixed = max(1, used // 4)
        moved = fixed + (places - fixed + rotation * (used - fixed)) % max(1, amount - fixed)
        return jnp.zeros((amount,), jnp.int32).at[order[jnp.where(places < fixed, places, moved)]].set(jnp.asarray(tallies, jnp.int32))

    tallies = jnp.where(number % 4 == 0, named(heavy_load, number // 4), named(usual, number - number // 4 - 1))
    mixed = jax.random.permutation(jax.random.fold_in(own, 3), amount)
    giver, receiver = mixed[0:amount // 2 * 2:2], mixed[1:amount // 2 * 2:2]
    room = jnp.minimum(tallies[giver] - 1, bound - tallies[receiver]) // 2
    room = jnp.where((giver == order[0]) | (receiver == order[0]) | (tallies[receiver] == 0), 0, jnp.maximum(room, 0))
    moved = jax.random.randint(jax.random.fold_in(own, 4), (amount // 2,), 0, 1 << 20) % (room + 1)
    tallies = tallies.at[giver].add(-moved).at[receiver].add(moved)
    labels = jnp.searchsorted(jnp.cumsum(tallies), jnp.arange(rows * top), side="right").astype(jnp.int32)
    table = labels.reshape(top, rows).T
    table = table[jax.random.permutation(jax.random.fold_in(own, 1), rows)]
    rotation = jax.random.randint(jax.random.fold_in(own, 2), (rows, 1), 0, top)
    return jnp.take_along_axis(table, (jnp.arange(top)[None, :] + rotation) % top, axis=1)


def load_shares(amount, total, reach, slope, full):
    weights = [(1 << 20) // math.isqrt(grade ** slope) + 1 for grade in range(1, amount + 1)]
    largest = reach if full else min(reach, max(-(-total // amount), total * weights[0] // sum(weights)))
    least = 1 if total - largest >= amount - 1 else 0
    given, rest = [largest] + [least] * (amount - 1), total - largest - least * (amount - 1)
    while rest > 0:
        movable = [i for i in range(1, amount) if given[i] < largest] or [i for i in range(1, amount) if given[i] < reach]
        pool, budget = sum([weights[i] for i in movable]), rest
        for i in movable:
            more = min(reach - given[i], max(1, budget * weights[i] // pool), rest)
            given[i] = given[i] + more
            rest = rest - more
    return np.array(given)


def gaussian(stream_key, extent, spread, limit, pieces=(), held_as=jnp.bfloat16):
    array = spread * jax.random.normal(stream_key, extent, jnp.float32)
    if pieces:
        array = array * levels(stream_key, extent, pieces, -0.22, 0.18)
    return jnp.clip(array, -limit, limit).astype(held_as)


def setup_inputs(seed: int = 0, part: int = 0) -> dict:
    keys = jax.random.split(jax.random.key(seed), 9)
    own_keys = jax.random.split(jax.random.fold_in(keys[8], part), 9)
    hidden = gaussian(own_keys[0], (ROWS, D), 1.0, 6.0, ((0, 8), (1, 2)))
    adapter_ids_keys = jax.random.split(jax.random.fold_in(own_keys[1], 1), ROWS // ROWS_DEV)
    adapter_ids_turns = jax.random.permutation(jax.random.fold_in(own_keys[1], 3), ROWS // ROWS_DEV)
    adapter_ids = jax.vmap(lambda own, number: shared_out(jax.random.fold_in(own_keys[1], 2), own, number, ROWS_DEV, ADAPTERS, 1, MOST, 2))(adapter_ids_keys, adapter_ids_turns).reshape((ROWS, 1))
    page_table = jax.random.permutation(keys[2], ADAPTERS).astype(jnp.int32)
    gate_weight = gaussian(keys[3], (D, FF_WIN), D ** -0.5, 0.0625, ((0, 2), (1, 8)))
    up_weight = gaussian(keys[4], (D, FF_WIN), D ** -0.5, 0.0625, ((0, 2), (1, 8)))
    shrink = gaussian(keys[5], (ADAPTERS, D, 2 * R), D ** -0.5, 0.0625, ((0, 8), (1, 2)))
    gate_expander_matrices = gaussian(keys[6], (ADAPTERS, R, FF_WIN), R ** -0.5, 1.0, ((2, 8),))
    up_expander_matrices = gaussian(keys[7], (ADAPTERS, R, FF_WIN), R ** -0.5, 1.0, ((2, 8),))
    return {"hidden": hidden, "adapter_ids": adapter_ids, "page_table": page_table, "gate_weight": gate_weight, "up_weight": up_weight, "shrink": shrink, "gate_expander_matrices": gate_expander_matrices, "up_expander_matrices": up_expander_matrices}


adapter_scale_factor = 0.5


def reference(hidden, adapter_ids, page_table, gate_weight, up_weight, shrink, gate_expander_matrices, up_expander_matrices):
    slot = page_table[adapter_ids[:, 0]].astype(jnp.int32)
    table = jnp.arange(ADAPTERS, dtype=jnp.int32)
    slot_hot = (slot[:, None] == table[None, :]).astype(jnp.float32)
    per_slot = jnp.einsum('rd,sdk->rsk', hidden.astype(jnp.float32), shrink.astype(jnp.float32))
    shrunk = jnp.einsum('rsk,rs->rk', per_slot, slot_hot).astype(jnp.bfloat16)
    gate_frozen_output = jnp.dot(hidden, gate_weight, preferred_element_type=jnp.float32)
    up_frozen_output = jnp.dot(hidden, up_weight, preferred_element_type=jnp.float32)
    shrunk_wide = shrunk.astype(jnp.float32)
    gate_in = (slot_hot[:, :, None] * shrunk_wide[:, None, :R]).reshape(ROWS, ADAPTERS * R)
    up_in = (slot_hot[:, :, None] * shrunk_wide[:, None, R:]).reshape(ROWS, ADAPTERS * R)
    gate_adapter_change = jnp.dot(gate_in, gate_expander_matrices.astype(jnp.float32).reshape(ADAPTERS * R, FF_WIN))
    up_adapter_change = jnp.dot(up_in, up_expander_matrices.astype(jnp.float32).reshape(ADAPTERS * R, FF_WIN))
    gate_preactivation = gate_frozen_output + adapter_scale_factor * gate_adapter_change
    up_preactivation = up_frozen_output + adapter_scale_factor * up_adapter_change
    return (jax.nn.silu(gate_preactivation) * up_preactivation).astype(jnp.bfloat16)
```

```python
import functools

import jax
import jax.numpy as jnp
from jax import lax
from jax.experimental import pallas as pl
from jax.experimental.pallas import tpu as pltpu
from jax.sharding import PartitionSpec as P

adapter_scale_factor = 0.5
LANES = 128
BLOCK = 256
LAG = 3
MESH = pl.DeviceIdType.MESH


def iota(shape, axis):
    return lax.broadcasted_iota(jnp.int32, shape, axis)


def fused_kernel(
    pool,
    ids_ref,
    table_ref,
    hidden_ref,
    gate_hbm,
    up_hbm,
    shrink_hbm,
    gate_expander_hbm,
    up_expander_hbm,
    out_ref,
    gathered,
    rows_in,
    gate_w,
    up_w,
    shrink_w,
    gate_expander,
    up_expander,
    partial,
    partner_partial,
    shrunk_partial,
    shrunk_partner,
    slot_own,
    slot_parts,
    gate_in,
    up_in,
    acted,
    land,
    local_sem,
    gather_send,
    gather_recv,
    shrunk_sem,
    slot_send,
    slot_recv,
    partial_send,
    partial_recv,
    act_send,
    act_recv,
    share_send,
    share_recv,
    out_sem,
):
    me = lax.axis_index("pool")
    core = lax.axis_index("tensor")
    other = 1 - core
    z, y = me // 2, me % 2
    depth = pool // 2
    half_pool = pool // 2
    own_rows, width = hidden_ref.shape
    rows = pool * own_rows
    half = rows // 2
    rank2 = shrink_w.shape[1]
    rank = rank2 // 2
    steps = partial.shape[0]
    stacked = gate_expander.shape[0]
    here = core == me // half_pool

    def local(i, src, dst):
        return pltpu.make_async_copy(src, dst, local_sem.at[i])

    loads = [
        local(0, shrink_hbm, shrink_w),
        local(1, gate_hbm, gate_w),
        local(2, up_hbm, up_w),
        local(3, gate_expander_hbm, gate_expander),
        local(4, up_expander_hbm, up_expander),
    ]
    for load in loads:
        load.start()

    adapters = table_ref.shape[1]
    id_hot = ids_ref[...] == iota((own_rows, adapters), 1)
    slot = jnp.sum(jnp.where(id_hot, table_ref[...], 0), axis=1, keepdims=True)
    hot = jnp.where(slot == iota((own_rows, LANES), 1), 1.0, 0.0).astype(jnp.bfloat16)
    gathered[me, :, :width] = hidden_ref[...]
    gathered[me, :, width:] = hot

    barrier = pltpu.get_barrier_semaphore()
    for step in range(1, pool):
        pl.semaphore_signal(
            barrier, inc=1, device_id={"pool": lax.rem(me + step, pool)}, device_id_type=MESH
        )
    pl.semaphore_signal(barrier, inc=1, device_id={"tensor": other}, device_id_type=MESH)
    pl.semaphore_wait(barrier, pool)

    def gather_copy(block, way, target):
        return pltpu.make_async_remote_copy(
            src_ref=gathered.at[block],
            dst_ref=gathered.at[block],
            send_sem=gather_send.at[way, block],
            recv_sem=gather_recv.at[block],
            device_id={"pool": target},
            device_id_type=MESH,
        )

    def block_of(level):
        return level * 2 + y

    def to_side(level):
        return gather_copy(block_of(level), 0, z * 2 + (1 - y))

    def to_above(level):
        return gather_copy(block_of(level), 1, (z + 1) * 2 + y)

    def to_below(level):
        return gather_copy(block_of(level), 2, (z - 1) * 2 + y)

    @pl.when(z < depth - 1)
    def _():
        to_above(z).start()

    @pl.when(z > 0)
    def _():
        to_below(z).start()

    to_side(z).start()

    def arrived(block):
        gather_copy(block, 0, me).wait_recv()

    for distance in range(1, depth):

        @pl.when(z - distance >= 0)
        def _():
            level = z - distance
            arrived(block_of(level))

            @pl.when(z < depth - 1)
            def _():
                to_above(level).start()

            to_side(level).start()

        @pl.when(z + distance < depth)
        def _():
            level = z + distance
            arrived(block_of(level))

            @pl.when(z > 0)
            def _():
                to_below(level).start()

            to_side(level).start()

    for level in range(depth):
        arrived(level * 2 + (1 - y))

    for pair in range(pool // 2):
        both = gathered[2 * pair : 2 * pair + 2].astype(jnp.float32)
        rows_in[2 * pair * own_rows : (2 * pair + 2) * own_rows, :] = both.reshape(
            2 * own_rows, width + LANES
        ).astype(jnp.bfloat16)

    loads[0].wait()
    shrunk_partial[...] = jnp.dot(
        rows_in[:, :width], shrink_w[...], preferred_element_type=jnp.float32
    )
    mine = pl.ds(pl.multiple_of(core * half, 16), half)
    theirs = pl.ds(pl.multiple_of(other * half, 16), half)
    shrunk_copy = pltpu.make_async_remote_copy(
        src_ref=shrunk_partial.at[theirs],
        dst_ref=shrunk_partner,
        send_sem=shrunk_sem.at[0],
        recv_sem=shrunk_sem.at[1],
        device_id={"tensor": other},
        device_id_type=MESH,
    )
    shrunk_copy.start()
    for load in loads[1:]:
        load.wait()

    def slot_copy(step):
        target = lax.rem(me + step, pool)
        return pltpu.make_async_remote_copy(
            src_ref=slot_own,
            dst_ref=slot_parts.at[step],
            send_sem=slot_send.at[step],
            recv_sem=slot_recv.at[step],
            device_id={"pool": target},
            device_id_type=MESH,
        )

    def share_shrunk():
        shrunk_copy.wait_recv()
        mask = jnp.sum(
            jnp.where(
                iota((half, LANES), 1) == me, rows_in[mine, width:].astype(jnp.float32), 0.0
            ),
            axis=1,
            keepdims=True,
        )
        total = (shrunk_partial[mine, :] + shrunk_partner[...]).astype(jnp.bfloat16)
        slot_own[...] = jnp.where(mask > 0.5, total.astype(jnp.float32), 0.0).astype(
            jnp.bfloat16
        )
        for step in range(1, pool):
            slot_copy(step).start()

    def spread_shrunk():
        total = slot_own[...].astype(jnp.float32)
        for step in range(1, pool):
            slot_copy(step).wait_recv()
            total = total + slot_parts[step].astype(jnp.float32)
        shrunk = total.astype(jnp.bfloat16)
        spread = jnp.where(
            iota((LANES, stacked), 1) // rank == iota((LANES, stacked), 0), 1.0, 0.0
        ).astype(jnp.bfloat16)
        hot_in = jnp.dot(rows_in[mine, width:], spread, preferred_element_type=jnp.float32)
        for offset, ref in ((0, gate_in), (rank, up_in)):
            repeat = jnp.where(
                iota((rank2, stacked), 1) % rank + offset == iota((rank2, stacked), 0), 1.0, 0.0
            ).astype(jnp.bfloat16)
            value = jnp.dot(shrunk, repeat, preferred_element_type=jnp.float32)
            ref[...] = (value * hot_in).astype(jnp.bfloat16)

    def partial_copy(c):
        return pltpu.make_async_remote_copy(
            src_ref=partial.at[c, :, theirs, :],
            dst_ref=partner_partial.at[c],
            send_sem=partial_send.at[c],
            recv_sem=partial_recv.at[c],
            device_id={"tensor": other},
            device_id_type=MESH,
        )

    def act_copy(c, j):
        target = core * half_pool + j
        return pltpu.make_async_remote_copy(
            src_ref=acted.at[c, j],
            dst_ref=land.at[c, me],
            send_sem=act_send.at[c, j],
            recv_sem=act_recv.at[c, me],
            device_id={"pool": target},
            device_id_type=MESH,
        )

    def columns_of(c):
        return pl.ds(pl.multiple_of(c * BLOCK, BLOCK), BLOCK)

    def project(c):
        columns = columns_of(c)
        for k, weight in enumerate((gate_w, up_w)):
            partial[c, k] = jnp.dot(
                rows_in[:, :width], weight[:, columns], preferred_element_type=jnp.float32
            )
        partial_copy(c).start()

    def activate(c):
        columns = columns_of(c)
        partial_copy(c).wait_recv()
        pre = []
        for k, (left, expander) in enumerate(((gate_in, gate_expander), (up_in, up_expander))):
            change = jnp.dot(
                left[...], expander[:, columns], preferred_element_type=jnp.float32
            )
            pre.append(
                partial[c, k, mine, :] + partner_partial[c, k] + adapter_scale_factor * change
            )
        gate, up = pre
        value = gate / (1.0 + jnp.exp(-gate)) * up
        value = value.reshape(half_pool, own_rows, BLOCK).astype(jnp.bfloat16)
        acted[c] = value
        for j in range(half_pool):
            is_own = core * half_pool + j == me

            @pl.when(jnp.logical_not(is_own))
            def _():
                act_copy(c, j).start()

            @pl.when(is_own)
            def _():
                land[c, me] = acted[c, j]

    def step_body(c, carry):
        project(c)

        @pl.when(c == 0)
        def _():
            share_shrunk()

        @pl.when(c == LAG)
        def _():
            spread_shrunk()

        @pl.when(c >= LAG)
        def _():
            activate(c - LAG)

        return carry

    lax.fori_loop(0, steps, step_body, 0)

    def late_body(c, carry):
        activate(c)
        return carry

    lax.fori_loop(steps - LAG, steps, late_body, 0)

    def share_copy(c):
        return pltpu.make_async_remote_copy(
            src_ref=land.at[c],
            dst_ref=land.at[c],
            send_sem=share_send.at[c],
            recv_sem=share_recv.at[c],
            device_id={"tensor": other},
            device_id_type=MESH,
        )

    def out_copy(c):
        return pltpu.make_async_copy(land.at[c], out_ref.at[c], out_sem.at[c])

    @pl.when(here)
    def _():
        def receive(c, carry):
            for step in range(1, pool):
                source = lax.rem(me + step, pool)
                pltpu.make_async_remote_copy(
                    src_ref=acted.at[c, 0],
                    dst_ref=land.at[c, source],
                    send_sem=act_send.at[c, 0],
                    recv_sem=act_recv.at[c, source],
                    device_id={"pool": source},
                    device_id_type=MESH,
                ).wait_recv()
            share_copy(c).start()
            out_copy(c).start()
            return carry

        lax.fori_loop(0, steps, receive, 0)

    @pl.when(jnp.logical_not(here))
    def _():
        def receive(c, carry):
            share_copy(c).wait_recv()
            out_copy(c).start()
            return carry

        lax.fori_loop(0, steps, receive, 0)

    def finish(c, carry):
        partial_copy(c).wait_send()
        for j in range(half_pool):

            @pl.when(core * half_pool + j != me)
            def _():
                act_copy(c, j).wait_send()

        @pl.when(here)
        def _():
            share_copy(c).wait_send()

        out_copy(c).wait()
        return carry

    lax.fori_loop(0, steps, finish, 0)
    shrunk_copy.wait_send()
    for step in range(1, pool):
        slot_copy(step).wait_send()
    for level in range(depth):
        to_side(level).wait_send()

        @pl.when(jnp.logical_and(level <= z, z < depth - 1))
        def _():
            to_above(level).wait_send()

        @pl.when(jnp.logical_and(level >= z, z > 0))
        def _():
            to_below(level).wait_send()


def fused_body(
    pool,
    hidden,
    adapter_ids,
    page_table,
    gate_weight,
    up_weight,
    shrink,
    gate_expander_matrices,
    up_expander_matrices,
):
    own_rows, width = hidden.shape
    columns = gate_weight.shape[1]
    rank2 = shrink.shape[2]
    steps = columns // BLOCK
    rows = pool * own_rows
    half = rows // 2
    half_pool = pool // 2
    stacked = gate_expander_matrices.shape[0] * gate_expander_matrices.shape[1]
    bf16, f32 = jnp.bfloat16, jnp.float32
    dma = pltpu.SemaphoreType.DMA
    vmem = pl.BlockSpec(memory_space=pltpu.VMEM)
    anywhere = pl.BlockSpec(memory_space=pl.ANY)
    result = pl.pallas_call(
        functools.partial(fused_kernel, pool),
        out_shape=jax.ShapeDtypeStruct((steps, pool, own_rows, BLOCK), bf16),
        in_specs=[vmem] * 3 + [anywhere] * 5,
        out_specs=anywhere,
        scratch_shapes=[
            pltpu.VMEM((pool, own_rows, width + LANES), bf16),
            pltpu.VMEM((rows, width + LANES), bf16),
            pltpu.VMEM((width, columns), bf16),
            pltpu.VMEM((width, columns), bf16),
            pltpu.VMEM((width, rank2), bf16),
            pltpu.VMEM((stacked, columns), bf16),
            pltpu.VMEM((stacked, columns), bf16),
            pltpu.VMEM((steps, 2, rows, BLOCK), f32),
            pltpu.VMEM((steps, 2, half, BLOCK), f32),
            pltpu.VMEM((rows, rank2), f32),
            pltpu.VMEM((half, rank2), f32),
            pltpu.VMEM((half, rank2), bf16),
            pltpu.VMEM((pool, half, rank2), bf16),
            pltpu.VMEM((half, stacked), bf16),
            pltpu.VMEM((half, stacked), bf16),
            pltpu.VMEM((steps, half_pool, own_rows, BLOCK), bf16),
            pltpu.VMEM((steps, pool, own_rows, BLOCK), bf16),
            dma((5,)),
            dma((3, pool)),
            dma((pool,)),
            dma((2,)),
            dma((pool,)),
            dma((pool,)),
            dma((steps,)),
            dma((steps,)),
            dma((steps, half_pool)),
            dma((steps, pool)),
            dma((steps,)),
            dma((steps,)),
            dma((steps,)),
        ],
        compiler_params=pltpu.CompilerParams(
            collective_id=0, has_side_effects=True, vmem_limit_bytes=56 * 1024 * 1024
        ),
        cost_estimate=pl.CostEstimate(
            flops=4 * rows * width * columns,
            bytes_accessed=4 * width * columns,
            transcendentals=half * columns,
        ),
    )(
        adapter_ids,
        page_table.reshape(1, -1),
        hidden,
        gate_weight,
        up_weight,
        shrink.reshape(width, rank2),
        gate_expander_matrices.reshape(stacked, columns),
        up_expander_matrices.reshape(stacked, columns),
    )
    return result.transpose(2, 1, 0, 3).reshape(own_rows, pool * columns)


def expansion_products(shrunk_part, hot_part, gate_expander_matrices, up_expander_matrices):
    rank = gate_expander_matrices.shape[1]
    number = hot_part.shape[0]
    width = gate_expander_matrices.shape[2]
    gate_in = (hot_part[:, :, None] * shrunk_part[:, None, :rank]).reshape(number, -1)
    up_in = (hot_part[:, :, None] * shrunk_part[:, None, rank:]).reshape(number, -1)
    gate_adapter_change = jnp.dot(
        gate_in, gate_expander_matrices.reshape(-1, width), preferred_element_type=jnp.float32
    )
    up_adapter_change = jnp.dot(
        up_in, up_expander_matrices.reshape(-1, width), preferred_element_type=jnp.float32
    )
    return jnp.concatenate([gate_adapter_change, up_adapter_change], axis=1)


def body(
    hidden,
    adapter_ids,
    page_table,
    gate_weight,
    up_weight,
    shrink,
    gate_expander_matrices,
    up_expander_matrices,
):
    adapters = page_table.shape[0]
    columns = gate_weight.shape[1]
    table = jnp.arange(adapters, dtype=jnp.int32)
    id_hot = adapter_ids == table[None, :]
    slot = jnp.sum(jnp.where(id_hot, page_table[None, :], 0), axis=1)
    slot_hot = (slot[:, None] == table[None, :]).astype(jnp.bfloat16)
    hot_piece = slot_hot.astype(jnp.float32)
    per_slot = jnp.einsum(
        "rd,sdk->rsk",
        hidden,
        lax.all_gather(shrink, "pool", axis=0, tiled=True),
        preferred_element_type=jnp.float32,
    )
    partial_value = jnp.einsum("rsk,rs->rk", per_slot, hot_piece, precision=lax.Precision.HIGHEST)
    shrunk = lax.psum(partial_value, "tensor").astype(jnp.bfloat16)
    piece = lax.all_gather(hidden, "pool", axis=0, tiled=True)
    gate_part = jnp.dot(piece, gate_weight, preferred_element_type=jnp.float32)
    up_part = jnp.dot(piece, up_weight, preferred_element_type=jnp.float32)
    base_part = jnp.concatenate([gate_part, up_part], axis=1)
    reduced_rows_gathered = lax.all_gather(shrunk, "pool", axis=0, tiled=True)
    slot_all = lax.all_gather(slot, "pool", axis=0, tiled=True)
    active_rows_gathered = (slot_all[:, None] == table[None, :]).astype(jnp.bfloat16)
    combined_sum = lax.psum(base_part, "tensor")
    combined_sum = combined_sum + adapter_scale_factor * expansion_products(
        reduced_rows_gathered, active_rows_gathered, gate_expander_matrices, up_expander_matrices
    )
    gate_preactivation = combined_sum[:, :columns]
    up_preactivation = combined_sum[:, columns:]
    activated = (jax.nn.silu(gate_preactivation) * up_preactivation).astype(jnp.bfloat16)
    return lax.all_to_all(activated, "pool", split_axis=0, concat_axis=1, tiled=True)


def chosen_body(pool, *args):
    hidden, _, page_table, gate_weight, _, shrink = args[:6]
    fits = (
        pool % 4 == 0
        and page_table.shape[0] == pool
        and shrink.shape[0] == 1
        and pool <= LANES
        and gate_weight.shape[1] % BLOCK == 0
        and gate_weight.shape[1] // BLOCK > LAG
        and hidden.shape[0] % 8 == 0
    )
    return fused_body(pool, *args) if fits else body(*args)


def solution(mesh):
    in_specs = (
        P(("groups", "pool"), "tensor"),
        P(("groups", "pool"), None),
        P(),
        P("tensor", "pool"),
        P("tensor", "pool"),
        P("pool", "tensor", None),
        P(None, None, "pool"),
        P(None, None, "pool"),
    )
    out_specs = P(("groups", "pool"), None)
    return jax.shard_map(
        functools.partial(chosen_body, mesh.shape["pool"]),
        mesh=mesh,
        in_specs=in_specs,
        out_specs=out_specs,
        check_vma=False,
    )
```

```python
import functools

import jax
import jax.numpy as jnp
from jax import lax
from jax.experimental import pallas as pl
from jax.experimental.pallas import tpu as pltpu
from jax.sharding import PartitionSpec as P

adapter_scale_factor = 0.5
LANES = 128
BLOCK = 256
LAG = 3
MESH = pl.DeviceIdType.MESH


def iota(shape, axis):
    return lax.broadcasted_iota(jnp.int32, shape, axis)


def dot_transposed(left, right):
    return lax.dot_general(
        left, right, (((1,), (1,)), ((), ())), preferred_element_type=jnp.float32
    )


def fused_kernel(
    pool,
    ids_ref,
    table_ref,
    hidden_ref,
    gate_hbm,
    up_hbm,
    shrink_hbm,
    gate_expander_hbm,
    up_expander_hbm,
    out_ref,
    gathered,
    rows_in,
    gate_w,
    up_w,
    shrink_w,
    gate_expander,
    up_expander,
    partial,
    partner_partial,
    shrunk_partial,
    shrunk_partner,
    slot_own,
    slot_parts,
    gate_in,
    up_in,
    acted,
    land,
    local_sem,
    gather_send,
    gather_recv,
    shrunk_sem,
    slot_send,
    slot_recv,
    partial_send,
    partial_recv,
    act_send,
    act_recv,
    share_send,
    share_recv,
):
    me = lax.axis_index("pool")
    core = lax.axis_index("tensor")
    other = 1 - core
    z, y = me // 2, me % 2
    depth = pool // 2
    half_pool = pool // 2
    own_rows, width = hidden_ref.shape
    rows = pool * own_rows
    half = rows // 2
    rank2 = shrink_w.shape[0]
    rank = rank2 // 2
    steps = partial.shape[0]
    stacked = gate_expander.shape[0]
    here = core == me // half_pool

    def local(i, src, dst):
        return pltpu.make_async_copy(src, dst, local_sem.at[i])

    loads = [
        local(0, shrink_hbm, shrink_w),
        local(1, gate_hbm, gate_w),
        local(2, up_hbm, up_w),
        local(3, gate_expander_hbm, gate_expander),
        local(4, up_expander_hbm, up_expander),
    ]
    for load in loads:
        load.start()

    ids = ids_ref[...]
    slot = jnp.zeros_like(ids)
    for adapter in range(pool):
        slot = jnp.where(ids == adapter, table_ref[adapter], slot)
    hot_columns = jnp.where(slot == iota((LANES, own_rows), 0), 1.0, 0.0).astype(jnp.bfloat16)
    unit = jnp.where(
        iota((own_rows, own_rows), 0) == iota((own_rows, own_rows), 1), 1.0, 0.0
    ).astype(jnp.bfloat16)
    hot = dot_transposed(unit, hot_columns).astype(jnp.bfloat16)
    gathered[me, :, :width] = hidden_ref[...]
    gathered[me, :, width:] = hot

    barrier = pltpu.get_barrier_semaphore()
    for step in range(1, pool):
        pl.semaphore_signal(
            barrier, inc=1, device_id={"pool": lax.rem(me + step, pool)}, device_id_type=MESH
        )
    pl.semaphore_signal(barrier, inc=1, device_id={"tensor": other}, device_id_type=MESH)
    pl.semaphore_wait(barrier, pool)

    def gather_copy(block, way, target):
        return pltpu.make_async_remote_copy(
            src_ref=gathered.at[block],
            dst_ref=gathered.at[block],
            send_sem=gather_send.at[way, block],
            recv_sem=gather_recv.at[block],
            device_id={"pool": target},
            device_id_type=MESH,
        )

    def block_of(level):
        return level * 2 + y

    def to_side(level):
        return gather_copy(block_of(level), 0, z * 2 + (1 - y))

    def to_above(level):
        return gather_copy(block_of(level), 1, (z + 1) * 2 + y)

    def to_below(level):
        return gather_copy(block_of(level), 2, (z - 1) * 2 + y)

    @pl.when(z < depth - 1)
    def _():
        to_above(z).start()

    @pl.when(z > 0)
    def _():
        to_below(z).start()

    to_side(z).start()

    def arrived(block):
        gather_copy(block, 0, me).wait_recv()

    for distance in range(1, depth):

        @pl.when(z - distance >= 0)
        def _():
            level = z - distance
            arrived(block_of(level))

            @pl.when(z < depth - 1)
            def _():
                to_above(level).start()

            to_side(level).start()

        @pl.when(z + distance < depth)
        def _():
            level = z + distance
            arrived(block_of(level))

            @pl.when(z > 0)
            def _():
                to_below(level).start()

            to_side(level).start()

    for level in range(depth):
        arrived(level * 2 + (1 - y))

    for pair in range(pool // 2):
        both = gathered[2 * pair : 2 * pair + 2].astype(jnp.float32)
        rows_in[2 * pair * own_rows : (2 * pair + 2) * own_rows, :] = both.reshape(
            2 * own_rows, width + LANES
        ).astype(jnp.bfloat16)

    loads[0].wait()
    shrunk_partial[...] = dot_transposed(rows_in[:, :width], shrink_w[...])
    mine = pl.ds(pl.multiple_of(core * half, 16), half)
    theirs = pl.ds(pl.multiple_of(other * half, 16), half)
    shrunk_copy = pltpu.make_async_remote_copy(
        src_ref=shrunk_partial.at[theirs],
        dst_ref=shrunk_partner,
        send_sem=shrunk_sem.at[0],
        recv_sem=shrunk_sem.at[1],
        device_id={"tensor": other},
        device_id_type=MESH,
    )
    shrunk_copy.start()
    for load in loads[1:]:
        load.wait()

    def slot_copy(step):
        target = lax.rem(me + step, pool)
        return pltpu.make_async_remote_copy(
            src_ref=slot_own,
            dst_ref=slot_parts.at[step],
            send_sem=slot_send.at[step],
            recv_sem=slot_recv.at[step],
            device_id={"pool": target},
            device_id_type=MESH,
        )

    def share_shrunk():
        shrunk_copy.wait_recv()
        mask = jnp.sum(
            jnp.where(
                iota((half, LANES), 1) == me, rows_in[mine, width:].astype(jnp.float32), 0.0
            ),
            axis=1,
            keepdims=True,
        )
        total = (shrunk_partial[mine, :] + shrunk_partner[...]).astype(jnp.bfloat16)
        slot_own[...] = jnp.where(mask > 0.5, total.astype(jnp.float32), 0.0).astype(
            jnp.bfloat16
        )
        for step in range(1, pool):
            slot_copy(step).start()

    def spread_shrunk():
        total = slot_own[...].astype(jnp.float32)
        for step in range(1, pool):
            slot_copy(step).wait_recv()
            total = total + slot_parts[step].astype(jnp.float32)
        shrunk = total.astype(jnp.bfloat16)
        spread = jnp.where(
            iota((LANES, stacked), 1) // rank == iota((LANES, stacked), 0), 1.0, 0.0
        ).astype(jnp.bfloat16)
        hot_in = jnp.dot(rows_in[mine, width:], spread, preferred_element_type=jnp.float32)
        for offset, ref in ((0, gate_in), (rank, up_in)):
            repeat = jnp.where(
                iota((rank2, stacked), 1) % rank + offset == iota((rank2, stacked), 0), 1.0, 0.0
            ).astype(jnp.bfloat16)
            value = jnp.dot(shrunk, repeat, preferred_element_type=jnp.float32)
            ref[...] = (value * hot_in).astype(jnp.bfloat16)

    def partial_copy(c):
        return pltpu.make_async_remote_copy(
            src_ref=partial.at[c, :, theirs, :],
            dst_ref=partner_partial.at[c],
            send_sem=partial_send.at[c],
            recv_sem=partial_recv.at[c],
            device_id={"tensor": other},
            device_id_type=MESH,
        )

    def act_copy(c, j):
        target = core * half_pool + j
        return pltpu.make_async_remote_copy(
            src_ref=acted.at[c, j],
            dst_ref=land.at[c, me],
            send_sem=act_send.at[c, j],
            recv_sem=act_recv.at[c, me],
            device_id={"pool": target},
            device_id_type=MESH,
        )

    def columns_of(c):
        return pl.ds(pl.multiple_of(c * BLOCK, BLOCK), BLOCK)

    def project(c):
        columns = columns_of(c)
        for k, weight in enumerate((gate_w, up_w)):
            partial[c, k] = jnp.dot(
                rows_in[:, :width], weight[:, columns], preferred_element_type=jnp.float32
            )
        partial_copy(c).start()

    def activate(c):
        columns = columns_of(c)
        partial_copy(c).wait_recv()
        pre = []
        for k, (left, expander) in enumerate(((gate_in, gate_expander), (up_in, up_expander))):
            change = jnp.dot(
                left[...], expander[:, columns], preferred_element_type=jnp.float32
            )
            pre.append(
                partial[c, k, mine, :] + partner_partial[c, k] + adapter_scale_factor * change
            )
        gate, up = pre
        value = gate / (1.0 + jnp.exp(-gate)) * up
        value = value.reshape(half_pool, own_rows, BLOCK).astype(jnp.bfloat16)
        acted[c] = value
        for j in range(half_pool):
            is_own = core * half_pool + j == me

            @pl.when(jnp.logical_not(is_own))
            def _():
                act_copy(c, j).start()

            @pl.when(is_own)
            def _():
                land[c, me] = acted[c, j]

    def step_body(c, carry):
        project(c)

        @pl.when(c == 0)
        def _():
            share_shrunk()

        @pl.when(c == LAG)
        def _():
            spread_shrunk()

        @pl.when(c >= LAG)
        def _():
            activate(c - LAG)

        return carry

    lax.fori_loop(0, steps, step_body, 0)

    def late_body(c, carry):
        activate(c)
        return carry

    lax.fori_loop(steps - LAG, steps, late_body, 0)

    def share_copy(c):
        return pltpu.make_async_remote_copy(
            src_ref=land.at[c],
            dst_ref=land.at[c],
            send_sem=share_send.at[c],
            recv_sem=share_recv.at[c],
            device_id={"tensor": other},
            device_id_type=MESH,
        )

    def place(c):
        for source in range(pool):
            column = pl.multiple_of((source * steps + c) * BLOCK, BLOCK)
            out_ref[:, pl.ds(column, BLOCK)] = land[c, source]

    @pl.when(here)
    def _():
        def receive(c, carry):
            for step in range(1, pool):
                source = lax.rem(me + step, pool)
                pltpu.make_async_remote_copy(
                    src_ref=acted.at[c, 0],
                    dst_ref=land.at[c, source],
                    send_sem=act_send.at[c, 0],
                    recv_sem=act_recv.at[c, source],
                    device_id={"pool": source},
                    device_id_type=MESH,
                ).wait_recv()
            share_copy(c).start()
            place(c)
            return carry

        lax.fori_loop(0, steps, receive, 0)

    @pl.when(jnp.logical_not(here))
    def _():
        def receive(c, carry):
            share_copy(c).wait_recv()
            place(c)
            return carry

        lax.fori_loop(0, steps, receive, 0)

    def finish(c, carry):
        partial_copy(c).wait_send()
        for j in range(half_pool):

            @pl.when(core * half_pool + j != me)
            def _():
                act_copy(c, j).wait_send()

        @pl.when(here)
        def _():
            share_copy(c).wait_send()

        return carry

    lax.fori_loop(0, steps, finish, 0)
    shrunk_copy.wait_send()
    for step in range(1, pool):
        slot_copy(step).wait_send()
    for level in range(depth):
        to_side(level).wait_send()

        @pl.when(jnp.logical_and(level <= z, z < depth - 1))
        def _():
            to_above(level).wait_send()

        @pl.when(jnp.logical_and(level >= z, z > 0))
        def _():
            to_below(level).wait_send()


def fused_body(
    pool,
    hidden,
    adapter_ids,
    page_table,
    gate_weight,
    up_weight,
    shrink,
    gate_expander_matrices,
    up_expander_matrices,
):
    own_rows, width = hidden.shape
    columns = gate_weight.shape[1]
    rank2 = shrink.shape[2]
    steps = columns // BLOCK
    rows = pool * own_rows
    half = rows // 2
    half_pool = pool // 2
    stacked = gate_expander_matrices.shape[0] * gate_expander_matrices.shape[1]
    bf16, f32 = jnp.bfloat16, jnp.float32
    dma = pltpu.SemaphoreType.DMA
    vmem = pl.BlockSpec(memory_space=pltpu.VMEM)
    anywhere = pl.BlockSpec(memory_space=pl.ANY)
    result = pl.pallas_call(
        functools.partial(fused_kernel, pool),
        out_shape=jax.ShapeDtypeStruct((own_rows, pool * columns), bf16),
        in_specs=[vmem, pl.BlockSpec(memory_space=pltpu.SMEM), vmem] + [anywhere] * 5,
        out_specs=vmem,
        scratch_shapes=[
            pltpu.VMEM((pool, own_rows, width + LANES), bf16),
            pltpu.VMEM((rows, width + LANES), bf16),
            pltpu.VMEM((width, columns), bf16),
            pltpu.VMEM((width, columns), bf16),
            pltpu.VMEM((rank2, width), bf16),
            pltpu.VMEM((stacked, columns), bf16),
            pltpu.VMEM((stacked, columns), bf16),
            pltpu.VMEM((steps, 2, rows, BLOCK), f32),
            pltpu.VMEM((steps, 2, half, BLOCK), f32),
            pltpu.VMEM((rows, rank2), f32),
            pltpu.VMEM((half, rank2), f32),
            pltpu.VMEM((half, rank2), bf16),
            pltpu.VMEM((pool, half, rank2), bf16),
            pltpu.VMEM((half, stacked), bf16),
            pltpu.VMEM((half, stacked), bf16),
            pltpu.VMEM((steps, half_pool, own_rows, BLOCK), bf16),
            pltpu.VMEM((steps, pool, own_rows, BLOCK), bf16),
            dma((5,)),
            dma((3, pool)),
            dma((pool,)),
            dma((2,)),
            dma((pool,)),
            dma((pool,)),
            dma((steps,)),
            dma((steps,)),
            dma((steps, half_pool)),
            dma((steps, pool)),
            dma((steps,)),
            dma((steps,)),
        ],
        compiler_params=pltpu.CompilerParams(
            collective_id=0, has_side_effects=True, vmem_limit_bytes=56 * 1024 * 1024
        ),
        cost_estimate=pl.CostEstimate(
            flops=4 * rows * width * columns,
            bytes_accessed=4 * width * columns,
            transcendentals=half * columns,
        ),
    )(
        adapter_ids.reshape(1, own_rows),
        page_table,
        hidden,
        gate_weight,
        up_weight,
        shrink.reshape(width, rank2).T,
        gate_expander_matrices.reshape(stacked, columns),
        up_expander_matrices.reshape(stacked, columns),
    )
    return result


def expansion_products(shrunk_part, hot_part, gate_expander_matrices, up_expander_matrices):
    rank = gate_expander_matrices.shape[1]
    number = hot_part.shape[0]
    width = gate_expander_matrices.shape[2]
    gate_in = (hot_part[:, :, None] * shrunk_part[:, None, :rank]).reshape(number, -1)
    up_in = (hot_part[:, :, None] * shrunk_part[:, None, rank:]).reshape(number, -1)
    gate_adapter_change = jnp.dot(
        gate_in, gate_expander_matrices.reshape(-1, width), preferred_element_type=jnp.float32
    )
    up_adapter_change = jnp.dot(
        up_in, up_expander_matrices.reshape(-1, width), preferred_element_type=jnp.float32
    )
    return jnp.concatenate([gate_adapter_change, up_adapter_change], axis=1)


def body(
    hidden,
    adapter_ids,
    page_table,
    gate_weight,
    up_weight,
    shrink,
    gate_expander_matrices,
    up_expander_matrices,
):
    adapters = page_table.shape[0]
    columns = gate_weight.shape[1]
    table = jnp.arange(adapters, dtype=jnp.int32)
    id_hot = adapter_ids == table[None, :]
    slot = jnp.sum(jnp.where(id_hot, page_table[None, :], 0), axis=1)
    slot_hot = (slot[:, None] == table[None, :]).astype(jnp.bfloat16)
    hot_piece = slot_hot.astype(jnp.float32)
    per_slot = jnp.einsum(
        "rd,sdk->rsk",
        hidden,
        lax.all_gather(shrink, "pool", axis=0, tiled=True),
        preferred_element_type=jnp.float32,
    )
    partial_value = jnp.einsum("rsk,rs->rk", per_slot, hot_piece, precision=lax.Precision.HIGHEST)
    shrunk = lax.psum(partial_value, "tensor").astype(jnp.bfloat16)
    piece = lax.all_gather(hidden, "pool", axis=0, tiled=True)
    gate_part = jnp.dot(piece, gate_weight, preferred_element_type=jnp.float32)
    up_part = jnp.dot(piece, up_weight, preferred_element_type=jnp.float32)
    base_part = jnp.concatenate([gate_part, up_part], axis=1)
    reduced_rows_gathered = lax.all_gather(shrunk, "pool", axis=0, tiled=True)
    slot_all = lax.all_gather(slot, "pool", axis=0, tiled=True)
    active_rows_gathered = (slot_all[:, None] == table[None, :]).astype(jnp.bfloat16)
    combined_sum = lax.psum(base_part, "tensor")
    combined_sum = combined_sum + adapter_scale_factor * expansion_products(
        reduced_rows_gathered, active_rows_gathered, gate_expander_matrices, up_expander_matrices
    )
    gate_preactivation = combined_sum[:, :columns]
    up_preactivation = combined_sum[:, columns:]
    activated = (jax.nn.silu(gate_preactivation) * up_preactivation).astype(jnp.bfloat16)
    return lax.all_to_all(activated, "pool", split_axis=0, concat_axis=1, tiled=True)


def chosen_body(pool, *args):
    hidden, _, page_table, gate_weight, _, shrink = args[:6]
    fits = (
        pool % 4 == 0
        and page_table.shape[0] == pool
        and shrink.shape[0] == 1
        and pool <= LANES
        and gate_weight.shape[1] % BLOCK == 0
        and gate_weight.shape[1] // BLOCK > LAG
        and hidden.shape[0] % 8 == 0
    )
    return fused_body(pool, *args) if fits else body(*args)


def solution(mesh):
    in_specs = (
        P(("groups", "pool"), "tensor"),
        P(("groups", "pool"), None),
        P(),
        P("tensor", "pool"),
        P("tensor", "pool"),
        P("pool", "tensor", None),
        P(None, None, "pool"),
        P(None, None, "pool"),
    )
    out_specs = P(("groups", "pool"), None)
    return jax.shard_map(
        functools.partial(chosen_body, mesh.shape["pool"]),
        mesh=mesh,
        in_specs=in_specs,
        out_specs=out_specs,
        check_vma=False,
    )
```

```python
import functools

import jax
import jax.numpy as jnp
from jax import lax
from jax.experimental import pallas as pl
from jax.experimental.pallas import tpu as pltpu
from jax.sharding import PartitionSpec as P

adapter_scale_factor = 0.5
LANES = 128
BLOCK = 256
PIECES = 3
LAG = 3
MESH = pl.DeviceIdType.MESH


def iota(shape, axis):
    return lax.broadcasted_iota(jnp.int32, shape, axis)


def dot_transposed(left, right):
    return lax.dot_general(
        left, right, (((1,), (1,)), ((), ())), preferred_element_type=jnp.float32
    )


def fused_kernel(
    pool,
    ids_ref,
    table_ref,
    hidden_ref,
    gate_hbm,
    up_hbm,
    shrink_hbm,
    gate_expander_hbm,
    up_expander_hbm,
    out_ref,
    gathered,
    rows_in,
    gate_w,
    up_w,
    shrink_w,
    gate_expander,
    up_expander,
    partial,
    partner_partial,
    shrunk_partial,
    shrunk_partner,
    slot_own,
    slot_parts,
    gate_in,
    up_in,
    acted,
    land,
    local_sem,
    gather_send,
    gather_recv,
    shrunk_sem,
    slot_send,
    slot_recv,
    partial_send,
    partial_recv,
    act_send,
    act_recv,
    share_send,
    share_recv,
):
    me = lax.axis_index("pool")
    core = lax.axis_index("tensor")
    other = 1 - core
    z, y = me // 2, me % 2
    depth = pool // 2
    half_pool = pool // 2
    own_rows, width = hidden_ref.shape
    rows = pool * own_rows
    half = rows // 2
    rank2 = shrink_w.shape[0]
    rank = rank2 // 2
    steps = partial.shape[0]
    stacked = gate_expander.shape[0]
    here = core == me // half_pool

    def local(i, src, dst):
        return pltpu.make_async_copy(src, dst, local_sem.at[i])

    loads = [
        local(0, shrink_hbm, shrink_w),
        local(1, gate_hbm, gate_w),
        local(2, up_hbm, up_w),
        local(3, gate_expander_hbm, gate_expander),
        local(4, up_expander_hbm, up_expander),
    ]
    for load in loads:
        load.start()

    ids = ids_ref[...]
    slot = jnp.zeros_like(ids)
    for adapter in range(pool):
        slot = jnp.where(ids == adapter, table_ref[adapter], slot)
    hot_columns = jnp.where(slot == iota((LANES, own_rows), 0), 1.0, 0.0).astype(jnp.bfloat16)
    unit = jnp.where(
        iota((own_rows, own_rows), 0) == iota((own_rows, own_rows), 1), 1.0, 0.0
    ).astype(jnp.bfloat16)
    hot = dot_transposed(unit, hot_columns).astype(jnp.bfloat16)
    gathered[me, :, :width] = hidden_ref[...]
    gathered[me, :, width:] = hot

    barrier = pltpu.get_barrier_semaphore()
    for step in range(1, pool):
        pl.semaphore_signal(
            barrier, inc=1, device_id={"pool": lax.rem(me + step, pool)}, device_id_type=MESH
        )
    pl.semaphore_signal(barrier, inc=1, device_id={"tensor": other}, device_id_type=MESH)
    pl.semaphore_wait(barrier, pool)

    def gather_copy(block, way, target, q):
        wide = gathered.shape[2] // PIECES
        piece = gathered.at[block, :, pl.ds(q * wide, wide)]
        return pltpu.make_async_remote_copy(
            src_ref=piece,
            dst_ref=piece,
            send_sem=gather_send.at[way, q, block],
            recv_sem=gather_recv.at[q, block],
            device_id={"pool": target},
            device_id_type=MESH,
        )

    def block_of(level):
        return level * 2 + y

    def to_side(level, q):
        return gather_copy(block_of(level), 0, z * 2 + (1 - y), q)

    def to_above(level, q):
        return gather_copy(block_of(level), 1, (z + 1) * 2 + y, q)

    def to_below(level, q):
        return gather_copy(block_of(level), 2, (z - 1) * 2 + y, q)

    near = z + 1 - 2 * (z % 2)
    last = PIECES - 1

    def across(level, q, act):
        if q < last:
            act(to_side(level, q))
        else:

            @pl.when(level != near)
            def _():
                act(to_side(level, q))

    def to_near():
        return gather_copy(z * 2 + (1 - y), 3, near * 2 + y, last)

    def arrived(block, q):
        gather_copy(block, 0, me, q).wait_recv()

    for q in range(PIECES):

        @pl.when(z < depth - 1)
        def _():
            to_above(z, q).start()

        @pl.when(z > 0)
        def _():
            to_below(z, q).start()

        to_side(z, q).start()

    for distance in range(1, depth):
        for q in range(PIECES):

            @pl.when(z - distance >= 0)
            def _():
                level = z - distance
                arrived(block_of(level), q)

                @pl.when(z < depth - 1)
                def _():
                    to_above(level, q).start()

                across(level, q, lambda copy: copy.start())

            @pl.when(z + distance < depth)
            def _():
                level = z + distance
                arrived(block_of(level), q)

                @pl.when(z > 0)
                def _():
                    to_below(level, q).start()

                across(level, q, lambda copy: copy.start())

    arrived(z * 2 + (1 - y), last)
    to_near().start()

    for order in range(depth):
        level = 2 * ((z // 2 + order // 2) % (depth // 2)) + (z + order) % 2
        for q in range(PIECES):
            if order > 0 or q < last:
                arrived(level * 2 + (1 - y), q)
        both = gathered[pl.ds(level * 2, 2)].astype(jnp.float32)
        start = pl.multiple_of(level * (2 * own_rows), 16)
        rows_in[pl.ds(start, 2 * own_rows), :] = both.reshape(
            2 * own_rows, width + LANES
        ).astype(jnp.bfloat16)

    loads[0].wait()
    shrunk_partial[...] = dot_transposed(rows_in[:, :width], shrink_w[...])
    mine = pl.ds(pl.multiple_of(core * half, 16), half)
    theirs = pl.ds(pl.multiple_of(other * half, 16), half)
    shrunk_copy = pltpu.make_async_remote_copy(
        src_ref=shrunk_partial.at[theirs],
        dst_ref=shrunk_partner,
        send_sem=shrunk_sem.at[0],
        recv_sem=shrunk_sem.at[1],
        device_id={"tensor": other},
        device_id_type=MESH,
    )
    shrunk_copy.start()
    for load in loads[1:]:
        load.wait()

    def slot_copy(step):
        target = lax.rem(me + step, pool)
        return pltpu.make_async_remote_copy(
            src_ref=slot_own,
            dst_ref=slot_parts.at[step],
            send_sem=slot_send.at[step],
            recv_sem=slot_recv.at[step],
            device_id={"pool": target},
            device_id_type=MESH,
        )

    def share_shrunk():
        shrunk_copy.wait_recv()
        mask = jnp.sum(
            jnp.where(
                iota((half, LANES), 1) == me, rows_in[mine, width:].astype(jnp.float32), 0.0
            ),
            axis=1,
            keepdims=True,
        )
        total = (shrunk_partial[mine, :] + shrunk_partner[...]).astype(jnp.bfloat16)
        slot_own[...] = jnp.where(mask > 0.5, total.astype(jnp.float32), 0.0).astype(
            jnp.bfloat16
        )
        for step in range(1, pool):
            slot_copy(step).start()

    def spread_shrunk():
        total = slot_own[...].astype(jnp.float32)
        for step in range(1, pool):
            slot_copy(step).wait_recv()
            total = total + slot_parts[step].astype(jnp.float32)
        shrunk = total.astype(jnp.bfloat16)
        spread = jnp.where(
            iota((LANES, stacked), 1) // rank == iota((LANES, stacked), 0), 1.0, 0.0
        ).astype(jnp.bfloat16)
        hot_in = jnp.dot(rows_in[mine, width:], spread, preferred_element_type=jnp.float32)
        for offset, ref in ((0, gate_in), (rank, up_in)):
            repeat = jnp.where(
                iota((rank2, stacked), 1) % rank + offset == iota((rank2, stacked), 0), 1.0, 0.0
            ).astype(jnp.bfloat16)
            value = jnp.dot(shrunk, repeat, preferred_element_type=jnp.float32)
            ref[...] = (value * hot_in).astype(jnp.bfloat16)

    def partial_copy(c):
        return pltpu.make_async_remote_copy(
            src_ref=partial.at[c, :, theirs, :],
            dst_ref=partner_partial.at[c],
            send_sem=partial_send.at[c],
            recv_sem=partial_recv.at[c],
            device_id={"tensor": other},
            device_id_type=MESH,
        )

    def act_copy(c, j):
        target = core * half_pool + j
        return pltpu.make_async_remote_copy(
            src_ref=acted.at[c, j],
            dst_ref=land.at[c, me],
            send_sem=act_send.at[c, j],
            recv_sem=act_recv.at[c, me],
            device_id={"pool": target},
            device_id_type=MESH,
        )

    def columns_of(c):
        return pl.ds(pl.multiple_of(c * BLOCK, BLOCK), BLOCK)

    def project(c):
        columns = columns_of(c)
        for k, weight in enumerate((gate_w, up_w)):
            partial[c, k] = jnp.dot(
                rows_in[:, :width], weight[:, columns], preferred_element_type=jnp.float32
            )
        partial_copy(c).start()

    def activate(c):
        columns = columns_of(c)
        partial_copy(c).wait_recv()
        pre = []
        for k, (left, expander) in enumerate(((gate_in, gate_expander), (up_in, up_expander))):
            change = jnp.dot(
                left[...], expander[:, columns], preferred_element_type=jnp.float32
            )
            pre.append(
                partial[c, k, mine, :] + partner_partial[c, k] + adapter_scale_factor * change
            )
        gate, up = pre
        value = gate / (1.0 + jnp.exp(-gate)) * up
        value = value.reshape(half_pool, own_rows, BLOCK).astype(jnp.bfloat16)
        acted[c] = value
        for j in range(half_pool):
            is_own = core * half_pool + j == me

            @pl.when(jnp.logical_not(is_own))
            def _():
                act_copy(c, j).start()

            @pl.when(is_own)
            def _():
                land[c, me] = acted[c, j]

    def step_body(c, carry):
        project(c)

        @pl.when(c == 0)
        def _():
            share_shrunk()

        @pl.when(c == LAG)
        def _():
            spread_shrunk()

        @pl.when(c >= LAG)
        def _():
            activate(c - LAG)

        return carry

    lax.fori_loop(0, steps, step_body, 0)

    def late_body(c, carry):
        activate(c)
        return carry

    lax.fori_loop(steps - LAG, steps, late_body, 0)

    def share_copy(c):
        return pltpu.make_async_remote_copy(
            src_ref=land.at[c],
            dst_ref=land.at[c],
            send_sem=share_send.at[c],
            recv_sem=share_recv.at[c],
            device_id={"tensor": other},
            device_id_type=MESH,
        )

    def place(c):
        for source in range(pool):
            column = pl.multiple_of((source * steps + c) * BLOCK, BLOCK)
            out_ref[:, pl.ds(column, BLOCK)] = land[c, source]

    @pl.when(here)
    def _():
        def receive(c, carry):
            for step in range(1, pool):
                source = lax.rem(me + step, pool)
                pltpu.make_async_remote_copy(
                    src_ref=acted.at[c, 0],
                    dst_ref=land.at[c, source],
                    send_sem=act_send.at[c, 0],
                    recv_sem=act_recv.at[c, source],
                    device_id={"pool": source},
                    device_id_type=MESH,
                ).wait_recv()
            share_copy(c).start()
            place(c)
            return carry

        lax.fori_loop(0, steps, receive, 0)

    @pl.when(jnp.logical_not(here))
    def _():
        def receive(c, carry):
            share_copy(c).wait_recv()
            place(c)
            return carry

        lax.fori_loop(0, steps, receive, 0)

    def finish(c, carry):
        partial_copy(c).wait_send()
        for j in range(half_pool):

            @pl.when(core * half_pool + j != me)
            def _():
                act_copy(c, j).wait_send()

        @pl.when(here)
        def _():
            share_copy(c).wait_send()

        return carry

    lax.fori_loop(0, steps, finish, 0)
    shrunk_copy.wait_send()
    for step in range(1, pool):
        slot_copy(step).wait_send()
    for level in range(depth):
        for q in range(PIECES):
            across(level, q, lambda copy: copy.wait_send())

            @pl.when(jnp.logical_and(level <= z, z < depth - 1))
            def _():
                to_above(level, q).wait_send()

            @pl.when(jnp.logical_and(level >= z, z > 0))
            def _():
                to_below(level, q).wait_send()

    to_near().wait_send()


def fused_body(
    pool,
    hidden,
    adapter_ids,
    page_table,
    gate_weight,
    up_weight,
    shrink,
    gate_expander_matrices,
    up_expander_matrices,
):
    own_rows, width = hidden.shape
    columns = gate_weight.shape[1]
    rank2 = shrink.shape[2]
    steps = columns // BLOCK
    rows = pool * own_rows
    half = rows // 2
    half_pool = pool // 2
    stacked = gate_expander_matrices.shape[0] * gate_expander_matrices.shape[1]
    bf16, f32 = jnp.bfloat16, jnp.float32
    dma = pltpu.SemaphoreType.DMA
    vmem = pl.BlockSpec(memory_space=pltpu.VMEM)
    anywhere = pl.BlockSpec(memory_space=pl.ANY)
    result = pl.pallas_call(
        functools.partial(fused_kernel, pool),
        out_shape=jax.ShapeDtypeStruct((own_rows, pool * columns), bf16),
        in_specs=[vmem, pl.BlockSpec(memory_space=pltpu.SMEM), vmem] + [anywhere] * 5,
        out_specs=vmem,
        scratch_shapes=[
            pltpu.VMEM((pool, own_rows, width + LANES), bf16),
            pltpu.VMEM((rows, width + LANES), bf16),
            pltpu.VMEM((width, columns), bf16),
            pltpu.VMEM((width, columns), bf16),
            pltpu.VMEM((rank2, width), bf16),
            pltpu.VMEM((stacked, columns), bf16),
            pltpu.VMEM((stacked, columns), bf16),
            pltpu.VMEM((steps, 2, rows, BLOCK), f32),
            pltpu.VMEM((steps, 2, half, BLOCK), f32),
            pltpu.VMEM((rows, rank2), f32),
            pltpu.VMEM((half, rank2), f32),
            pltpu.VMEM((half, rank2), bf16),
            pltpu.VMEM((pool, half, rank2), bf16),
            pltpu.VMEM((half, stacked), bf16),
            pltpu.VMEM((half, stacked), bf16),
            pltpu.VMEM((steps, half_pool, own_rows, BLOCK), bf16),
            pltpu.VMEM((steps, pool, own_rows, BLOCK), bf16),
            dma((5,)),
            dma((4, PIECES, pool)),
            dma((PIECES, pool)),
            dma((2,)),
            dma((pool,)),
            dma((pool,)),
            dma((steps,)),
            dma((steps,)),
            dma((steps, half_pool)),
            dma((steps, pool)),
            dma((steps,)),
            dma((steps,)),
        ],
        compiler_params=pltpu.CompilerParams(
            collective_id=0, has_side_effects=True, vmem_limit_bytes=56 * 1024 * 1024
        ),
        cost_estimate=pl.CostEstimate(
            flops=4 * rows * width * columns,
            bytes_accessed=4 * width * columns,
            transcendentals=half * columns,
        ),
    )(
        adapter_ids.reshape(1, own_rows),
        page_table,
        hidden,
        gate_weight,
        up_weight,
        shrink.reshape(width, rank2).T,
        gate_expander_matrices.reshape(stacked, columns),
        up_expander_matrices.reshape(stacked, columns),
    )
    return result


def expansion_products(shrunk_part, hot_part, gate_expander_matrices, up_expander_matrices):
    rank = gate_expander_matrices.shape[1]
    number = hot_part.shape[0]
    width = gate_expander_matrices.shape[2]
    gate_in = (hot_part[:, :, None] * shrunk_part[:, None, :rank]).reshape(number, -1)
    up_in = (hot_part[:, :, None] * shrunk_part[:, None, rank:]).reshape(number, -1)
    gate_adapter_change = jnp.dot(
        gate_in, gate_expander_matrices.reshape(-1, width), preferred_element_type=jnp.float32
    )
    up_adapter_change = jnp.dot(
        up_in, up_expander_matrices.reshape(-1, width), preferred_element_type=jnp.float32
    )
    return jnp.concatenate([gate_adapter_change, up_adapter_change], axis=1)


def body(
    hidden,
    adapter_ids,
    page_table,
    gate_weight,
    up_weight,
    shrink,
    gate_expander_matrices,
    up_expander_matrices,
):
    adapters = page_table.shape[0]
    columns = gate_weight.shape[1]
    table = jnp.arange(adapters, dtype=jnp.int32)
    id_hot = adapter_ids == table[None, :]
    slot = jnp.sum(jnp.where(id_hot, page_table[None, :], 0), axis=1)
    slot_hot = (slot[:, None] == table[None, :]).astype(jnp.bfloat16)
    hot_piece = slot_hot.astype(jnp.float32)
    per_slot = jnp.einsum(
        "rd,sdk->rsk",
        hidden,
        lax.all_gather(shrink, "pool", axis=0, tiled=True),
        preferred_element_type=jnp.float32,
    )
    partial_value = jnp.einsum("rsk,rs->rk", per_slot, hot_piece, precision=lax.Precision.HIGHEST)
    shrunk = lax.psum(partial_value, "tensor").astype(jnp.bfloat16)
    piece = lax.all_gather(hidden, "pool", axis=0, tiled=True)
    gate_part = jnp.dot(piece, gate_weight, preferred_element_type=jnp.float32)
    up_part = jnp.dot(piece, up_weight, preferred_element_type=jnp.float32)
    base_part = jnp.concatenate([gate_part, up_part], axis=1)
    reduced_rows_gathered = lax.all_gather(shrunk, "pool", axis=0, tiled=True)
    slot_all = lax.all_gather(slot, "pool", axis=0, tiled=True)
    active_rows_gathered = (slot_all[:, None] == table[None, :]).astype(jnp.bfloat16)
    combined_sum = lax.psum(base_part, "tensor")
    combined_sum = combined_sum + adapter_scale_factor * expansion_products(
        reduced_rows_gathered, active_rows_gathered, gate_expander_matrices, up_expander_matrices
    )
    gate_preactivation = combined_sum[:, :columns]
    up_preactivation = combined_sum[:, columns:]
    activated = (jax.nn.silu(gate_preactivation) * up_preactivation).astype(jnp.bfloat16)
    return lax.all_to_all(activated, "pool", split_axis=0, concat_axis=1, tiled=True)


def chosen_body(pool, *args):
    hidden, _, page_table, gate_weight, _, shrink = args[:6]
    fits = (
        pool % 4 == 0
        and page_table.shape[0] == pool
        and shrink.shape[0] == 1
        and pool <= LANES
        and gate_weight.shape[1] % BLOCK == 0
        and gate_weight.shape[1] // BLOCK > LAG
        and hidden.shape[0] % 8 == 0
        and (hidden.shape[1] + LANES) % (PIECES * LANES) == 0
    )
    return fused_body(pool, *args) if fits else body(*args)


def solution(mesh):
    in_specs = (
        P(("groups", "pool"), "tensor"),
        P(("groups", "pool"), None),
        P(),
        P("tensor", "pool"),
        P("tensor", "pool"),
        P("pool", "tensor", None),
        P(None, None, "pool"),
        P(None, None, "pool"),
    )
    out_specs = P(("groups", "pool"), None)
    return jax.shard_map(
        functools.partial(chosen_body, mesh.shape["pool"]),
        mesh=mesh,
        in_specs=in_specs,
        out_specs=out_specs,
        check_vma=False,
    )
```

```python
import functools

import jax
import jax.numpy as jnp
from jax import lax
from jax.experimental import pallas as pl
from jax.experimental.pallas import tpu as pltpu
from jax.sharding import PartitionSpec as P

adapter_scale_factor = 0.5
LANES = 128
BLOCK = 256
PIECES = 3
LAG = 2
MESH = pl.DeviceIdType.MESH


def iota(shape, axis):
    return lax.broadcasted_iota(jnp.int32, shape, axis)


def dot_transposed(left, right):
    return lax.dot_general(
        left, right, (((1,), (1,)), ((), ())), preferred_element_type=jnp.float32
    )


def fused_kernel(
    pool,
    ids_ref,
    table_ref,
    hidden_ref,
    gate_hbm,
    up_hbm,
    shrink_hbm,
    gate_expander_hbm,
    up_expander_hbm,
    out_ref,
    gathered,
    rows_in,
    gate_w,
    up_w,
    shrink_w,
    gate_expander,
    up_expander,
    partial,
    partner_partial,
    shrunk_partial,
    shrunk_partner,
    slot_own,
    slot_parts,
    gate_in,
    up_in,
    acted,
    land,
    local_sem,
    gather_send,
    gather_recv,
    shrunk_sem,
    slot_send,
    slot_recv,
    partial_send,
    partial_recv,
    act_send,
    act_recv,
    share_send,
    share_recv,
):
    me = lax.axis_index("pool")
    core = lax.axis_index("tensor")
    other = 1 - core
    z, y = me // 2, me % 2
    depth = pool // 2
    half_pool = pool // 2
    own_rows, width = hidden_ref.shape
    rows = pool * own_rows
    half = rows // 2
    rank2 = shrink_w.shape[0]
    rank = rank2 // 2
    steps = partial.shape[0]
    stacked = gate_expander.shape[0]
    here = core == me // half_pool

    def local(i, src, dst):
        return pltpu.make_async_copy(src, dst, local_sem.at[i])

    loads = [
        local(0, shrink_hbm, shrink_w),
        local(1, gate_hbm, gate_w),
        local(2, up_hbm, up_w),
        local(3, gate_expander_hbm, gate_expander),
        local(4, up_expander_hbm, up_expander),
    ]
    for load in loads:
        load.start()

    ids = ids_ref[...]
    slot = jnp.zeros_like(ids)
    for adapter in range(pool):
        slot = jnp.where(ids == adapter, table_ref[adapter], slot)
    hot_columns = jnp.where(slot == iota((LANES, own_rows), 0), 1.0, 0.0).astype(jnp.bfloat16)
    unit = jnp.where(
        iota((own_rows, own_rows), 0) == iota((own_rows, own_rows), 1), 1.0, 0.0
    ).astype(jnp.bfloat16)
    hot = dot_transposed(unit, hot_columns).astype(jnp.bfloat16)
    gathered[me, :, :width] = hidden_ref[...]
    gathered[me, :, width:] = hot

    barrier = pltpu.get_barrier_semaphore()
    for step in range(1, pool):
        pl.semaphore_signal(
            barrier, inc=1, device_id={"pool": lax.rem(me + step, pool)}, device_id_type=MESH
        )
    pl.semaphore_signal(barrier, inc=1, device_id={"tensor": other}, device_id_type=MESH)
    pl.semaphore_wait(barrier, pool)

    def gather_copy(block, way, target, q):
        wide = gathered.shape[2] // PIECES
        piece = gathered.at[block, :, pl.ds(q * wide, wide)]
        return pltpu.make_async_remote_copy(
            src_ref=piece,
            dst_ref=piece,
            send_sem=gather_send.at[way, q, block],
            recv_sem=gather_recv.at[q, block],
            device_id={"pool": target},
            device_id_type=MESH,
        )

    def block_of(level):
        return level * 2 + y

    def to_side(level, q):
        return gather_copy(block_of(level), 0, z * 2 + (1 - y), q)

    def to_above(level, q):
        return gather_copy(block_of(level), 1, (z + 1) * 2 + y, q)

    def to_below(level, q):
        return gather_copy(block_of(level), 2, (z - 1) * 2 + y, q)

    near = z + 1 - 2 * (z % 2)
    last = PIECES - 1

    def across(level, q, act):
        if q < last:
            act(to_side(level, q))
        else:

            @pl.when(level != near)
            def _():
                act(to_side(level, q))

    def to_near():
        return gather_copy(z * 2 + (1 - y), 3, near * 2 + y, last)

    def arrived(block, q):
        gather_copy(block, 0, me, q).wait_recv()

    for q in range(PIECES):

        @pl.when(z < depth - 1)
        def _():
            to_above(z, q).start()

        @pl.when(z > 0)
        def _():
            to_below(z, q).start()

        to_side(z, q).start()

    def take(order):
        level = 2 * ((z // 2 + order // 2) % (depth // 2)) + (z + order) % 2
        for q in range(PIECES):
            arrived(level * 2 + (1 - y), q)
        both = gathered[pl.ds(level * 2, 2)].astype(jnp.float32)
        both = both.reshape(2 * own_rows, width + LANES).astype(jnp.bfloat16)
        taken = pl.ds(pl.multiple_of(level * (2 * own_rows), 16), 2 * own_rows)
        rows_in[taken, :] = both
        shrunk_partial[taken, :] = dot_transposed(both[:, :width], shrink_w[...])

    for distance in range(1, depth):
        for q in range(PIECES):

            @pl.when(z - distance >= 0)
            def _():
                level = z - distance
                arrived(block_of(level), q)

                @pl.when(z < depth - 1)
                def _():
                    to_above(level, q).start()

                across(level, q, lambda copy: copy.start())

            @pl.when(z + distance < depth)
            def _():
                level = z + distance
                arrived(block_of(level), q)

                @pl.when(z > 0)
                def _():
                    to_below(level, q).start()

                across(level, q, lambda copy: copy.start())

        if distance == 1:
            loads[0].wait()
            take(0)

    to_near().start()
    for order in range(1, depth):
        take(order)

    mine = pl.ds(pl.multiple_of(core * half, 16), half)
    theirs = pl.ds(pl.multiple_of(other * half, 16), half)
    shrunk_copy = pltpu.make_async_remote_copy(
        src_ref=shrunk_partial.at[theirs],
        dst_ref=shrunk_partner,
        send_sem=shrunk_sem.at[0],
        recv_sem=shrunk_sem.at[1],
        device_id={"tensor": other},
        device_id_type=MESH,
    )
    shrunk_copy.start()
    for load in loads[1:]:
        load.wait()

    def slot_copy(step):
        target = lax.rem(me + step, pool)
        return pltpu.make_async_remote_copy(
            src_ref=slot_own,
            dst_ref=slot_parts.at[step],
            send_sem=slot_send.at[step],
            recv_sem=slot_recv.at[step],
            device_id={"pool": target},
            device_id_type=MESH,
        )

    def share_shrunk():
        shrunk_copy.wait_recv()
        mask = jnp.sum(
            jnp.where(
                iota((half, LANES), 1) == me, rows_in[mine, width:].astype(jnp.float32), 0.0
            ),
            axis=1,
            keepdims=True,
        )
        total = (shrunk_partial[mine, :] + shrunk_partner[...]).astype(jnp.bfloat16)
        slot_own[...] = jnp.where(mask > 0.5, total.astype(jnp.float32), 0.0).astype(
            jnp.bfloat16
        )
        for step in range(1, pool):
            slot_copy(step).start()

    def spread_shrunk():
        total = slot_own[...].astype(jnp.float32)
        for step in range(1, pool):
            slot_copy(step).wait_recv()
            total = total + slot_parts[step].astype(jnp.float32)
        shrunk = total.astype(jnp.bfloat16)
        spread = jnp.where(
            iota((LANES, stacked), 1) // rank == iota((LANES, stacked), 0), 1.0, 0.0
        ).astype(jnp.bfloat16)
        hot_in = jnp.dot(rows_in[mine, width:], spread, preferred_element_type=jnp.float32)
        for offset, ref in ((0, gate_in), (rank, up_in)):
            repeat = jnp.where(
                iota((rank2, stacked), 1) % rank + offset == iota((rank2, stacked), 0), 1.0, 0.0
            ).astype(jnp.bfloat16)
            value = jnp.dot(shrunk, repeat, preferred_element_type=jnp.float32)
            ref[...] = (value * hot_in).astype(jnp.bfloat16)

    def partial_copy(c):
        return pltpu.make_async_remote_copy(
            src_ref=partial.at[c, :, theirs, :],
            dst_ref=partner_partial.at[c],
            send_sem=partial_send.at[c],
            recv_sem=partial_recv.at[c],
            device_id={"tensor": other},
            device_id_type=MESH,
        )

    def act_copy(c, j):
        target = core * half_pool + j
        return pltpu.make_async_remote_copy(
            src_ref=acted.at[c, j],
            dst_ref=land.at[c, me],
            send_sem=act_send.at[c, j],
            recv_sem=act_recv.at[c, me],
            device_id={"pool": target},
            device_id_type=MESH,
        )

    def columns_of(c):
        return pl.ds(pl.multiple_of(c * BLOCK, BLOCK), BLOCK)

    def project(c):
        columns = columns_of(c)
        for k, weight in enumerate((gate_w, up_w)):
            partial[c, k] = jnp.dot(
                rows_in[:, :width], weight[:, columns], preferred_element_type=jnp.float32
            )
        partial_copy(c).start()

    def activate(c):
        columns = columns_of(c)
        partial_copy(c).wait_recv()
        pre = []
        for k, (left, expander) in enumerate(((gate_in, gate_expander), (up_in, up_expander))):
            change = jnp.dot(
                left[...], expander[:, columns], preferred_element_type=jnp.float32
            )
            pre.append(
                partial[c, k, mine, :] + partner_partial[c, k] + adapter_scale_factor * change
            )
        gate, up = pre
        value = gate / (1.0 + jnp.exp(-gate)) * up
        value = value.reshape(half_pool, own_rows, BLOCK).astype(jnp.bfloat16)
        acted[c] = value
        for j in range(half_pool):
            is_own = core * half_pool + j == me

            @pl.when(jnp.logical_not(is_own))
            def _():
                act_copy(c, j).start()

            @pl.when(is_own)
            def _():
                land[c, me] = acted[c, j]

    def step_body(c, carry):
        project(c)

        @pl.when(c == 0)
        def _():
            share_shrunk()

        @pl.when(c == LAG)
        def _():
            spread_shrunk()

        @pl.when(c >= LAG)
        def _():
            activate(c - LAG)

        return carry

    lax.fori_loop(0, steps, step_body, 0)

    def late_body(c, carry):
        activate(c)
        return carry

    lax.fori_loop(steps - LAG, steps, late_body, 0)

    def share_copy(c):
        return pltpu.make_async_remote_copy(
            src_ref=land.at[c],
            dst_ref=land.at[c],
            send_sem=share_send.at[c],
            recv_sem=share_recv.at[c],
            device_id={"tensor": other},
            device_id_type=MESH,
        )

    def place(c):
        for source in range(pool):
            column = pl.multiple_of((source * steps + c) * BLOCK, BLOCK)
            out_ref[:, pl.ds(column, BLOCK)] = land[c, source]

    @pl.when(here)
    def _():
        def receive(c, carry):
            for step in range(1, pool):
                source = lax.rem(me + step, pool)
                pltpu.make_async_remote_copy(
                    src_ref=acted.at[c, 0],
                    dst_ref=land.at[c, source],
                    send_sem=act_send.at[c, 0],
                    recv_sem=act_recv.at[c, source],
                    device_id={"pool": source},
                    device_id_type=MESH,
                ).wait_recv()
            share_copy(c).start()
            place(c)
            return carry

        lax.fori_loop(0, steps, receive, 0)

    @pl.when(jnp.logical_not(here))
    def _():
        def receive(c, carry):
            share_copy(c).wait_recv()
            place(c)
            return carry

        lax.fori_loop(0, steps, receive, 0)

    def finish(c, carry):
        partial_copy(c).wait_send()
        for j in range(half_pool):

            @pl.when(core * half_pool + j != me)
            def _():
                act_copy(c, j).wait_send()

        @pl.when(here)
        def _():
            share_copy(c).wait_send()

        return carry

    lax.fori_loop(0, steps, finish, 0)
    shrunk_copy.wait_send()
    for step in range(1, pool):
        slot_copy(step).wait_send()
    for level in range(depth):
        for q in range(PIECES):
            across(level, q, lambda copy: copy.wait_send())

            @pl.when(jnp.logical_and(level <= z, z < depth - 1))
            def _():
                to_above(level, q).wait_send()

            @pl.when(jnp.logical_and(level >= z, z > 0))
            def _():
                to_below(level, q).wait_send()

    to_near().wait_send()


def fused_body(
    pool,
    hidden,
    adapter_ids,
    page_table,
    gate_weight,
    up_weight,
    shrink,
    gate_expander_matrices,
    up_expander_matrices,
):
    own_rows, width = hidden.shape
    columns = gate_weight.shape[1]
    rank2 = shrink.shape[2]
    steps = columns // BLOCK
    rows = pool * own_rows
    half = rows // 2
    half_pool = pool // 2
    stacked = gate_expander_matrices.shape[0] * gate_expander_matrices.shape[1]
    bf16, f32 = jnp.bfloat16, jnp.float32
    dma = pltpu.SemaphoreType.DMA
    vmem = pl.BlockSpec(memory_space=pltpu.VMEM)
    anywhere = pl.BlockSpec(memory_space=pl.ANY)
    result = pl.pallas_call(
        functools.partial(fused_kernel, pool),
        out_shape=jax.ShapeDtypeStruct((own_rows, pool * columns), bf16),
        in_specs=[vmem, pl.BlockSpec(memory_space=pltpu.SMEM), vmem] + [anywhere] * 5,
        out_specs=vmem,
        scratch_shapes=[
            pltpu.VMEM((pool, own_rows, width + LANES), bf16),
            pltpu.VMEM((rows, width + LANES), bf16),
            pltpu.VMEM((width, columns), bf16),
            pltpu.VMEM((width, columns), bf16),
            pltpu.VMEM((rank2, width), bf16),
            pltpu.VMEM((stacked, columns), bf16),
            pltpu.VMEM((stacked, columns), bf16),
            pltpu.VMEM((steps, 2, rows, BLOCK), f32),
            pltpu.VMEM((steps, 2, half, BLOCK), f32),
            pltpu.VMEM((rows, rank2), f32),
            pltpu.VMEM((half, rank2), f32),
            pltpu.VMEM((half, rank2), bf16),
            pltpu.VMEM((pool, half, rank2), bf16),
            pltpu.VMEM((half, stacked), bf16),
            pltpu.VMEM((half, stacked), bf16),
            pltpu.VMEM((steps, half_pool, own_rows, BLOCK), bf16),
            pltpu.VMEM((steps, pool, own_rows, BLOCK), bf16),
            dma((5,)),
            dma((4, PIECES, pool)),
            dma((PIECES, pool)),
            dma((2,)),
            dma((pool,)),
            dma((pool,)),
            dma((steps,)),
            dma((steps,)),
            dma((steps, half_pool)),
            dma((steps, pool)),
            dma((steps,)),
            dma((steps,)),
        ],
        compiler_params=pltpu.CompilerParams(
            collective_id=0, has_side_effects=True, vmem_limit_bytes=56 * 1024 * 1024
        ),
        cost_estimate=pl.CostEstimate(
            flops=4 * rows * width * columns,
            bytes_accessed=4 * width * columns,
            transcendentals=half * columns,
        ),
    )(
        adapter_ids.reshape(1, own_rows),
        page_table,
        hidden,
        gate_weight,
        up_weight,
        shrink.reshape(width, rank2).T,
        gate_expander_matrices.reshape(stacked, columns),
        up_expander_matrices.reshape(stacked, columns),
    )
    return result


def expansion_products(shrunk_part, hot_part, gate_expander_matrices, up_expander_matrices):
    rank = gate_expander_matrices.shape[1]
    number = hot_part.shape[0]
    width = gate_expander_matrices.shape[2]
    gate_in = (hot_part[:, :, None] * shrunk_part[:, None, :rank]).reshape(number, -1)
    up_in = (hot_part[:, :, None] * shrunk_part[:, None, rank:]).reshape(number, -1)
    gate_adapter_change = jnp.dot(
        gate_in, gate_expander_matrices.reshape(-1, width), preferred_element_type=jnp.float32
    )
    up_adapter_change = jnp.dot(
        up_in, up_expander_matrices.reshape(-1, width), preferred_element_type=jnp.float32
    )
    return jnp.concatenate([gate_adapter_change, up_adapter_change], axis=1)


def body(
    hidden,
    adapter_ids,
    page_table,
    gate_weight,
    up_weight,
    shrink,
    gate_expander_matrices,
    up_expander_matrices,
):
    adapters = page_table.shape[0]
    columns = gate_weight.shape[1]
    table = jnp.arange(adapters, dtype=jnp.int32)
    id_hot = adapter_ids == table[None, :]
    slot = jnp.sum(jnp.where(id_hot, page_table[None, :], 0), axis=1)
    slot_hot = (slot[:, None] == table[None, :]).astype(jnp.bfloat16)
    hot_piece = slot_hot.astype(jnp.float32)
    per_slot = jnp.einsum(
        "rd,sdk->rsk",
        hidden,
        lax.all_gather(shrink, "pool", axis=0, tiled=True),
        preferred_element_type=jnp.float32,
    )
    partial_value = jnp.einsum("rsk,rs->rk", per_slot, hot_piece, precision=lax.Precision.HIGHEST)
    shrunk = lax.psum(partial_value, "tensor").astype(jnp.bfloat16)
    piece = lax.all_gather(hidden, "pool", axis=0, tiled=True)
    gate_part = jnp.dot(piece, gate_weight, preferred_element_type=jnp.float32)
    up_part = jnp.dot(piece, up_weight, preferred_element_type=jnp.float32)
    base_part = jnp.concatenate([gate_part, up_part], axis=1)
    reduced_rows_gathered = lax.all_gather(shrunk, "pool", axis=0, tiled=True)
    slot_all = lax.all_gather(slot, "pool", axis=0, tiled=True)
    active_rows_gathered = (slot_all[:, None] == table[None, :]).astype(jnp.bfloat16)
    combined_sum = lax.psum(base_part, "tensor")
    combined_sum = combined_sum + adapter_scale_factor * expansion_products(
        reduced_rows_gathered, active_rows_gathered, gate_expander_matrices, up_expander_matrices
    )
    gate_preactivation = combined_sum[:, :columns]
    up_preactivation = combined_sum[:, columns:]
    activated = (jax.nn.silu(gate_preactivation) * up_preactivation).astype(jnp.bfloat16)
    return lax.all_to_all(activated, "pool", split_axis=0, concat_axis=1, tiled=True)


def chosen_body(pool, *args):
    hidden, _, page_table, gate_weight, _, shrink = args[:6]
    fits = (
        pool % 4 == 0
        and page_table.shape[0] == pool
        and shrink.shape[0] == 1
        and pool <= LANES
        and gate_weight.shape[1] % BLOCK == 0
        and gate_weight.shape[1] // BLOCK > LAG
        and hidden.shape[0] % 8 == 0
        and (hidden.shape[1] + LANES) % (PIECES * LANES) == 0
    )
    return fused_body(pool, *args) if fits else body(*args)


def solution(mesh):
    in_specs = (
        P(("groups", "pool"), "tensor"),
        P(("groups", "pool"), None),
        P(),
        P("tensor", "pool"),
        P("tensor", "pool"),
        P("pool", "tensor", None),
        P(None, None, "pool"),
        P(None, None, "pool"),
    )
    out_specs = P(("groups", "pool"), None)
    return jax.shard_map(
        functools.partial(chosen_body, mesh.shape["pool"]),
        mesh=mesh,
        in_specs=in_specs,
        out_specs=out_specs,
        check_vma=False,
    )
```

```python
import functools

import jax
import jax.numpy as jnp
from jax import lax
from jax.experimental import pallas as pl
from jax.experimental.pallas import tpu as pltpu
from jax.sharding import PartitionSpec as P

adapter_scale_factor = 0.5
LANES = 128
BLOCK = 256
PIECES = 3
LAG = 4
MESH = pl.DeviceIdType.MESH


def iota(shape, axis):
    return lax.broadcasted_iota(jnp.int32, shape, axis)


def dot_transposed(left, right):
    return lax.dot_general(
        left, right, (((1,), (1,)), ((), ())), preferred_element_type=jnp.float32
    )


def fused_kernel(
    pool,
    ids_ref,
    table_ref,
    hidden_ref,
    gate_hbm,
    up_hbm,
    shrink_hbm,
    gate_expander_hbm,
    up_expander_hbm,
    out_ref,
    gathered,
    rows_in,
    gate_w,
    up_w,
    shrink_w,
    gate_expander,
    up_expander,
    partial,
    partner_partial,
    shrunk_partial,
    shrunk_partner,
    slot_own,
    slot_parts,
    gate_in,
    up_in,
    acted,
    land,
    local_sem,
    gather_send,
    gather_recv,
    shrunk_sem,
    slot_send,
    slot_recv,
    partial_send,
    partial_recv,
    act_send,
    act_recv,
    share_send,
    share_recv,
):
    me = lax.axis_index("pool")
    core = lax.axis_index("tensor")
    other = 1 - core
    z, y = me // 2, me % 2
    depth = pool // 2
    half_pool = pool // 2
    own_rows, width = hidden_ref.shape
    rows = pool * own_rows
    half = rows // 2
    rank2 = shrink_w.shape[0]
    rank = rank2 // 2
    steps = partial.shape[0]
    stacked = gate_expander.shape[0]
    here = core == me // half_pool

    def local(i, src, dst):
        return pltpu.make_async_copy(src, dst, local_sem.at[i])

    loads = [
        local(0, shrink_hbm, shrink_w),
        local(1, gate_hbm, gate_w),
        local(2, up_hbm, up_w),
        local(3, gate_expander_hbm, gate_expander),
        local(4, up_expander_hbm, up_expander),
    ]
    for load in loads:
        load.start()

    ids = ids_ref[...]
    slot = jnp.zeros_like(ids)
    for adapter in range(pool):
        slot = jnp.where(ids == adapter, table_ref[adapter], slot)
    hot_columns = jnp.where(slot == iota((LANES, own_rows), 0), 1.0, 0.0).astype(jnp.bfloat16)
    unit = jnp.where(
        iota((own_rows, own_rows), 0) == iota((own_rows, own_rows), 1), 1.0, 0.0
    ).astype(jnp.bfloat16)
    hot = dot_transposed(unit, hot_columns).astype(jnp.bfloat16)
    gathered[me, :, :width] = hidden_ref[...]
    gathered[me, :, width:] = hot

    barrier = pltpu.get_barrier_semaphore()
    for step in range(1, pool):
        pl.semaphore_signal(
            barrier, inc=1, device_id={"pool": lax.rem(me + step, pool)}, device_id_type=MESH
        )
    pl.semaphore_signal(barrier, inc=1, device_id={"tensor": other}, device_id_type=MESH)
    pl.semaphore_wait(barrier, pool)

    def gather_copy(block, way, target, q):
        wide = gathered.shape[2] // PIECES
        piece = gathered.at[block, :, pl.ds(q * wide, wide)]
        return pltpu.make_async_remote_copy(
            src_ref=piece,
            dst_ref=piece,
            send_sem=gather_send.at[way, q, block],
            recv_sem=gather_recv.at[q, block],
            device_id={"pool": target},
            device_id_type=MESH,
        )

    def block_of(level):
        return level * 2 + y

    def to_side(level, q):
        return gather_copy(block_of(level), 0, z * 2 + (1 - y), q)

    def to_above(level, q):
        return gather_copy(block_of(level), 1, (z + 1) * 2 + y, q)

    def to_below(level, q):
        return gather_copy(block_of(level), 2, (z - 1) * 2 + y, q)

    near = z + 1 - 2 * (z % 2)
    last = PIECES - 1

    def across(level, q, act):
        if q < last:
            act(to_side(level, q))
        else:

            @pl.when(level != near)
            def _():
                act(to_side(level, q))

    def to_near():
        return gather_copy(z * 2 + (1 - y), 3, near * 2 + y, last)

    def arrived(block, q):
        gather_copy(block, 0, me, q).wait_recv()

    for q in range(PIECES):

        @pl.when(z < depth - 1)
        def _():
            to_above(z, q).start()

        @pl.when(z > 0)
        def _():
            to_below(z, q).start()

        to_side(z, q).start()

    def take(order):
        level = 2 * ((z // 2 + order // 2) % (depth // 2)) + (z + order) % 2
        for q in range(PIECES):
            arrived(level * 2 + (1 - y), q)
        both = gathered[pl.ds(level * 2, 2)].astype(jnp.float32)
        both = both.reshape(2 * own_rows, width + LANES).astype(jnp.bfloat16)
        taken = pl.ds(pl.multiple_of(level * (2 * own_rows), 16), 2 * own_rows)
        rows_in[taken, :] = both
        shrunk_partial[taken, :] = dot_transposed(both[:, :width], shrink_w[...])

    for distance in range(1, depth):
        for q in range(PIECES):

            @pl.when(z - distance >= 0)
            def _():
                level = z - distance
                arrived(block_of(level), q)

                @pl.when(z < depth - 1)
                def _():
                    to_above(level, q).start()

                across(level, q, lambda copy: copy.start())

            @pl.when(z + distance < depth)
            def _():
                level = z + distance
                arrived(block_of(level), q)

                @pl.when(z > 0)
                def _():
                    to_below(level, q).start()

                across(level, q, lambda copy: copy.start())

        if distance == 1:
            loads[0].wait()
            take(0)

    to_near().start()
    for order in range(1, depth):
        take(order)

    mine = pl.ds(pl.multiple_of(core * half, 16), half)
    theirs = pl.ds(pl.multiple_of(other * half, 16), half)
    shrunk_copy = pltpu.make_async_remote_copy(
        src_ref=shrunk_partial.at[theirs],
        dst_ref=shrunk_partner,
        send_sem=shrunk_sem.at[0],
        recv_sem=shrunk_sem.at[1],
        device_id={"tensor": other},
        device_id_type=MESH,
    )
    shrunk_copy.start()
    for load in loads[1:]:
        load.wait()

    def slot_copy(step):
        target = lax.rem(me + step, pool)
        return pltpu.make_async_remote_copy(
            src_ref=slot_own,
            dst_ref=slot_parts.at[step],
            send_sem=slot_send.at[step],
            recv_sem=slot_recv.at[step],
            device_id={"pool": target},
            device_id_type=MESH,
        )

    def share_shrunk():
        shrunk_copy.wait_recv()
        mask = jnp.sum(
            jnp.where(
                iota((half, LANES), 1) == me, rows_in[mine, width:].astype(jnp.float32), 0.0
            ),
            axis=1,
            keepdims=True,
        )
        total = (shrunk_partial[mine, :] + shrunk_partner[...]).astype(jnp.bfloat16)
        slot_own[...] = jnp.where(mask > 0.5, total.astype(jnp.float32), 0.0).astype(
            jnp.bfloat16
        )
        for step in range(1, pool):
            slot_copy(step).start()

    def spread_shrunk():
        total = slot_own[...].astype(jnp.float32)
        for step in range(1, pool):
            slot_copy(step).wait_recv()
            total = total + slot_parts[step].astype(jnp.float32)
        shrunk = total.astype(jnp.bfloat16)
        spread = jnp.where(
            iota((LANES, stacked), 1) // rank == iota((LANES, stacked), 0), 1.0, 0.0
        ).astype(jnp.bfloat16)
        hot_in = jnp.dot(rows_in[mine, width:], spread, preferred_element_type=jnp.float32)
        for offset, ref in ((0, gate_in), (rank, up_in)):
            repeat = jnp.where(
                iota((rank2, stacked), 1) % rank + offset == iota((rank2, stacked), 0), 1.0, 0.0
            ).astype(jnp.bfloat16)
            value = jnp.dot(shrunk, repeat, preferred_element_type=jnp.float32)
            ref[...] = (value * hot_in).astype(jnp.bfloat16)

    def partial_copy(c):
        return pltpu.make_async_remote_copy(
            src_ref=partial.at[c, :, theirs, :],
            dst_ref=partner_partial.at[c],
            send_sem=partial_send.at[c],
            recv_sem=partial_recv.at[c],
            device_id={"tensor": other},
            device_id_type=MESH,
        )

    def act_copy(c, j):
        target = core * half_pool + j
        return pltpu.make_async_remote_copy(
            src_ref=acted.at[c, j],
            dst_ref=land.at[c, me],
            send_sem=act_send.at[c, j],
            recv_sem=act_recv.at[c, me],
            device_id={"pool": target},
            device_id_type=MESH,
        )

    def columns_of(c):
        return pl.ds(pl.multiple_of(c * BLOCK, BLOCK), BLOCK)

    def project(c):
        columns = columns_of(c)
        for k, weight in enumerate((gate_w, up_w)):
            partial[c, k] = jnp.dot(
                rows_in[:, :width], weight[:, columns], preferred_element_type=jnp.float32
            )
        partial_copy(c).start()

    def activate(c):
        columns = columns_of(c)
        partial_copy(c).wait_recv()
        pre = []
        for k, (left, expander) in enumerate(((gate_in, gate_expander), (up_in, up_expander))):
            change = jnp.dot(
                left[...], expander[:, columns], preferred_element_type=jnp.float32
            )
            pre.append(
                partial[c, k, mine, :] + partner_partial[c, k] + adapter_scale_factor * change
            )
        gate, up = pre
        value = gate / (1.0 + jnp.exp(-gate)) * up
        value = value.reshape(half_pool, own_rows, BLOCK).astype(jnp.bfloat16)
        acted[c] = value
        for j in range(half_pool):
            is_own = core * half_pool + j == me

            @pl.when(jnp.logical_not(is_own))
            def _():
                act_copy(c, j).start()

            @pl.when(is_own)
            def _():
                land[c, me] = acted[c, j]

    def step_body(c, carry):
        project(c)

        @pl.when(c == 0)
        def _():
            share_shrunk()

        @pl.when(c == LAG)
        def _():
            spread_shrunk()

        @pl.when(c >= LAG)
        def _():
            activate(c - LAG)

        return carry

    lax.fori_loop(0, steps, step_body, 0)

    def late_body(c, carry):
        activate(c)
        return carry

    lax.fori_loop(steps - LAG, steps, late_body, 0)

    def share_copy(c):
        return pltpu.make_async_remote_copy(
            src_ref=land.at[c],
            dst_ref=land.at[c],
            send_sem=share_send.at[c],
            recv_sem=share_recv.at[c],
            device_id={"tensor": other},
            device_id_type=MESH,
        )

    def place(c):
        for source in range(pool):
            column = pl.multiple_of((source * steps + c) * BLOCK, BLOCK)
            out_ref[:, pl.ds(column, BLOCK)] = land[c, source]

    @pl.when(here)
    def _():
        def receive(c, carry):
            for step in range(1, pool):
                source = lax.rem(me + step, pool)
                pltpu.make_async_remote_copy(
                    src_ref=acted.at[c, 0],
                    dst_ref=land.at[c, source],
                    send_sem=act_send.at[c, 0],
                    recv_sem=act_recv.at[c, source],
                    device_id={"pool": source},
                    device_id_type=MESH,
                ).wait_recv()
            share_copy(c).start()
            place(c)
            return carry

        lax.fori_loop(0, steps, receive, 0)

    @pl.when(jnp.logical_not(here))
    def _():
        def receive(c, carry):
            share_copy(c).wait_recv()
            place(c)
            return carry

        lax.fori_loop(0, steps, receive, 0)

    def finish(c, carry):
        partial_copy(c).wait_send()
        for j in range(half_pool):

            @pl.when(core * half_pool + j != me)
            def _():
                act_copy(c, j).wait_send()

        @pl.when(here)
        def _():
            share_copy(c).wait_send()

        return carry

    lax.fori_loop(0, steps, finish, 0)
    shrunk_copy.wait_send()
    for step in range(1, pool):
        slot_copy(step).wait_send()
    for level in range(depth):
        for q in range(PIECES):
            across(level, q, lambda copy: copy.wait_send())

            @pl.when(jnp.logical_and(level <= z, z < depth - 1))
            def _():
                to_above(level, q).wait_send()

            @pl.when(jnp.logical_and(level >= z, z > 0))
            def _():
                to_below(level, q).wait_send()

    to_near().wait_send()


def fused_body(
    pool,
    hidden,
    adapter_ids,
    page_table,
    gate_weight,
    up_weight,
    shrink,
    gate_expander_matrices,
    up_expander_matrices,
):
    own_rows, width = hidden.shape
    columns = gate_weight.shape[1]
    rank2 = shrink.shape[2]
    steps = columns // BLOCK
    rows = pool * own_rows
    half = rows // 2
    half_pool = pool // 2
    stacked = gate_expander_matrices.shape[0] * gate_expander_matrices.shape[1]
    bf16, f32 = jnp.bfloat16, jnp.float32
    dma = pltpu.SemaphoreType.DMA
    vmem = pl.BlockSpec(memory_space=pltpu.VMEM)
    anywhere = pl.BlockSpec(memory_space=pl.ANY)
    result = pl.pallas_call(
        functools.partial(fused_kernel, pool),
        out_shape=jax.ShapeDtypeStruct((own_rows, pool * columns), bf16),
        in_specs=[vmem, pl.BlockSpec(memory_space=pltpu.SMEM), vmem] + [anywhere] * 5,
        out_specs=vmem,
        scratch_shapes=[
            pltpu.VMEM((pool, own_rows, width + LANES), bf16),
            pltpu.VMEM((rows, width + LANES), bf16),
            pltpu.VMEM((width, columns), bf16),
            pltpu.VMEM((width, columns), bf16),
            pltpu.VMEM((rank2, width), bf16),
            pltpu.VMEM((stacked, columns), bf16),
            pltpu.VMEM((stacked, columns), bf16),
            pltpu.VMEM((steps, 2, rows, BLOCK), f32),
            pltpu.VMEM((steps, 2, half, BLOCK), f32),
            pltpu.VMEM((rows, rank2), f32),
            pltpu.VMEM((half, rank2), f32),
            pltpu.VMEM((half, rank2), bf16),
            pltpu.VMEM((pool, half, rank2), bf16),
            pltpu.VMEM((half, stacked), bf16),
            pltpu.VMEM((half, stacked), bf16),
            pltpu.VMEM((steps, half_pool, own_rows, BLOCK), bf16),
            pltpu.VMEM((steps, pool, own_rows, BLOCK), bf16),
            dma((5,)),
            dma((4, PIECES, pool)),
            dma((PIECES, pool)),
            dma((2,)),
            dma((pool,)),
            dma((pool,)),
            dma((steps,)),
            dma((steps,)),
            dma((steps, half_pool)),
            dma((steps, pool)),
            dma((steps,)),
            dma((steps,)),
        ],
        compiler_params=pltpu.CompilerParams(
            collective_id=0, has_side_effects=True, vmem_limit_bytes=56 * 1024 * 1024
        ),
        cost_estimate=pl.CostEstimate(
            flops=4 * rows * width * columns,
            bytes_accessed=4 * width * columns,
            transcendentals=half * columns,
        ),
    )(
        adapter_ids.reshape(1, own_rows),
        page_table,
        hidden,
        gate_weight,
        up_weight,
        shrink.reshape(width, rank2).T,
        gate_expander_matrices.reshape(stacked, columns),
        up_expander_matrices.reshape(stacked, columns),
    )
    return result


def expansion_products(shrunk_part, hot_part, gate_expander_matrices, up_expander_matrices):
    rank = gate_expander_matrices.shape[1]
    number = hot_part.shape[0]
    width = gate_expander_matrices.shape[2]
    gate_in = (hot_part[:, :, None] * shrunk_part[:, None, :rank]).reshape(number, -1)
    up_in = (hot_part[:, :, None] * shrunk_part[:, None, rank:]).reshape(number, -1)
    gate_adapter_change = jnp.dot(
        gate_in, gate_expander_matrices.reshape(-1, width), preferred_element_type=jnp.float32
    )
    up_adapter_change = jnp.dot(
        up_in, up_expander_matrices.reshape(-1, width), preferred_element_type=jnp.float32
    )
    return jnp.concatenate([gate_adapter_change, up_adapter_change], axis=1)


def body(
    hidden,
    adapter_ids,
    page_table,
    gate_weight,
    up_weight,
    shrink,
    gate_expander_matrices,
    up_expander_matrices,
):
    adapters = page_table.shape[0]
    columns = gate_weight.shape[1]
    table = jnp.arange(adapters, dtype=jnp.int32)
    id_hot = adapter_ids == table[None, :]
    slot = jnp.sum(jnp.where(id_hot, page_table[None, :], 0), axis=1)
    slot_hot = (slot[:, None] == table[None, :]).astype(jnp.bfloat16)
    hot_piece = slot_hot.astype(jnp.float32)
    per_slot = jnp.einsum(
        "rd,sdk->rsk",
        hidden,
        lax.all_gather(shrink, "pool", axis=0, tiled=True),
        preferred_element_type=jnp.float32,
    )
    partial_value = jnp.einsum("rsk,rs->rk", per_slot, hot_piece, precision=lax.Precision.HIGHEST)
    shrunk = lax.psum(partial_value, "tensor").astype(jnp.bfloat16)
    piece = lax.all_gather(hidden, "pool", axis=0, tiled=True)
    gate_part = jnp.dot(piece, gate_weight, preferred_element_type=jnp.float32)
    up_part = jnp.dot(piece, up_weight, preferred_element_type=jnp.float32)
    base_part = jnp.concatenate([gate_part, up_part], axis=1)
    reduced_rows_gathered = lax.all_gather(shrunk, "pool", axis=0, tiled=True)
    slot_all = lax.all_gather(slot, "pool", axis=0, tiled=True)
    active_rows_gathered = (slot_all[:, None] == table[None, :]).astype(jnp.bfloat16)
    combined_sum = lax.psum(base_part, "tensor")
    combined_sum = combined_sum + adapter_scale_factor * expansion_products(
        reduced_rows_gathered, active_rows_gathered, gate_expander_matrices, up_expander_matrices
    )
    gate_preactivation = combined_sum[:, :columns]
    up_preactivation = combined_sum[:, columns:]
    activated = (jax.nn.silu(gate_preactivation) * up_preactivation).astype(jnp.bfloat16)
    return lax.all_to_all(activated, "pool", split_axis=0, concat_axis=1, tiled=True)


def chosen_body(pool, *args):
    hidden, _, page_table, gate_weight, _, shrink = args[:6]
    fits = (
        pool % 4 == 0
        and page_table.shape[0] == pool
        and shrink.shape[0] == 1
        and pool <= LANES
        and gate_weight.shape[1] % BLOCK == 0
        and gate_weight.shape[1] // BLOCK > LAG
        and hidden.shape[0] % 8 == 0
        and (hidden.shape[1] + LANES) % (PIECES * LANES) == 0
    )
    return fused_body(pool, *args) if fits else body(*args)


def solution(mesh):
    in_specs = (
        P(("groups", "pool"), "tensor"),
        P(("groups", "pool"), None),
        P(),
        P("tensor", "pool"),
        P("tensor", "pool"),
        P("pool", "tensor", None),
        P(None, None, "pool"),
        P(None, None, "pool"),
    )
    out_specs = P(("groups", "pool"), None)
    return jax.shard_map(
        functools.partial(chosen_body, mesh.shape["pool"]),
        mesh=mesh,
        in_specs=in_specs,
        out_specs=out_specs,
        check_vma=False,
    )
```

```python
import functools

import jax
import jax.numpy as jnp
from jax import lax
from jax.experimental import pallas as pl
from jax.experimental.pallas import tpu as pltpu
from jax.sharding import PartitionSpec as P

adapter_scale_factor = 0.5
LANES = 128
BLOCK = 256
PIECES = 3
LAG = 4
MESH = pl.DeviceIdType.MESH


def iota(shape, axis):
    return lax.broadcasted_iota(jnp.int32, shape, axis)


def dot_transposed(left, right):
    return lax.dot_general(
        left, right, (((1,), (1,)), ((), ())), preferred_element_type=jnp.float32
    )


def fused_kernel(
    pool,
    ids_ref,
    table_ref,
    hidden_ref,
    gate_hbm,
    up_hbm,
    shrink_hbm,
    gate_expander_hbm,
    up_expander_hbm,
    out_ref,
    gathered,
    rows_in,
    gate_w,
    up_w,
    shrink_w,
    gate_expander,
    up_expander,
    partial,
    partner_partial,
    shrunk_partial,
    shrunk_partner,
    slot_own,
    slot_parts,
    gate_in,
    up_in,
    acted,
    land,
    local_sem,
    gather_send,
    gather_recv,
    shrunk_sem,
    slot_send,
    slot_recv,
    partial_send,
    partial_recv,
    act_send,
    act_recv,
    share_send,
    share_recv,
):
    me = lax.axis_index("pool")
    core = lax.axis_index("tensor")
    other = 1 - core
    z, y = me // 2, me % 2
    depth = pool // 2
    half_pool = pool // 2
    own_rows, width = hidden_ref.shape
    rows = pool * own_rows
    half = rows // 2
    rank2 = shrink_w.shape[0]
    rank = rank2 // 2
    steps = partial.shape[0]
    stacked = gate_expander.shape[0]
    here = core == me // half_pool

    barrier = pltpu.get_barrier_semaphore()
    for step in range(1, pool):
        pl.semaphore_signal(
            barrier, inc=1, device_id={"pool": lax.rem(me + step, pool)}, device_id_type=MESH
        )
    pl.semaphore_signal(barrier, inc=1, device_id={"tensor": other}, device_id_type=MESH)

    def local(i, src, dst):
        return pltpu.make_async_copy(src, dst, local_sem.at[i])

    loads = [
        local(0, shrink_hbm, shrink_w),
        local(1, gate_hbm, gate_w),
        local(2, up_hbm, up_w),
        local(3, gate_expander_hbm, gate_expander),
        local(4, up_expander_hbm, up_expander),
    ]
    for load in loads:
        load.start()

    ids = ids_ref[...]
    slot = jnp.zeros_like(ids)
    for adapter in range(pool):
        slot = jnp.where(ids == adapter, table_ref[adapter], slot)
    hot_columns = jnp.where(slot == iota((LANES, own_rows), 0), 1.0, 0.0).astype(jnp.bfloat16)
    unit = jnp.where(
        iota((own_rows, own_rows), 0) == iota((own_rows, own_rows), 1), 1.0, 0.0
    ).astype(jnp.bfloat16)
    hot = dot_transposed(unit, hot_columns).astype(jnp.bfloat16)
    gathered[me, :, :width] = hidden_ref[...]
    gathered[me, :, width:] = hot

    pl.semaphore_wait(barrier, pool)

    def gather_copy(block, way, target, q):
        wide = gathered.shape[2] // PIECES
        piece = gathered.at[block, :, pl.ds(q * wide, wide)]
        return pltpu.make_async_remote_copy(
            src_ref=piece,
            dst_ref=piece,
            send_sem=gather_send.at[way, q, block],
            recv_sem=gather_recv.at[q, block],
            device_id={"pool": target},
            device_id_type=MESH,
        )

    def block_of(level):
        return level * 2 + y

    def to_side(level, q):
        return gather_copy(block_of(level), 0, z * 2 + (1 - y), q)

    def to_above(level, q):
        return gather_copy(block_of(level), 1, (z + 1) * 2 + y, q)

    def to_below(level, q):
        return gather_copy(block_of(level), 2, (z - 1) * 2 + y, q)

    near = z + 1 - 2 * (z % 2)
    last = PIECES - 1

    def across(level, q, act):
        if q < last:
            act(to_side(level, q))
        else:

            @pl.when(level != near)
            def _():
                act(to_side(level, q))

    def to_near():
        return gather_copy(z * 2 + (1 - y), 3, near * 2 + y, last)

    def arrived(block, q):
        gather_copy(block, 0, me, q).wait_recv()

    for q in range(PIECES):

        @pl.when(z < depth - 1)
        def _():
            to_above(z, q).start()

        @pl.when(z > 0)
        def _():
            to_below(z, q).start()

        to_side(z, q).start()

    def take(order):
        level = 2 * ((z // 2 + order // 2) % (depth // 2)) + (z + order) % 2
        for q in range(PIECES):
            arrived(level * 2 + (1 - y), q)
        both = gathered[pl.ds(level * 2, 2)].astype(jnp.float32)
        both = both.reshape(2 * own_rows, width + LANES).astype(jnp.bfloat16)
        taken = pl.ds(pl.multiple_of(level * (2 * own_rows), 16), 2 * own_rows)
        rows_in[taken, :] = both
        shrunk_partial[taken, :] = dot_transposed(both[:, :width], shrink_w[...])

    for distance in range(1, depth):
        for q in range(PIECES):

            @pl.when(z - distance >= 0)
            def _():
                level = z - distance
                arrived(block_of(level), q)

                @pl.when(z < depth - 1)
                def _():
                    to_above(level, q).start()

                across(level, q, lambda copy: copy.start())

            @pl.when(z + distance < depth)
            def _():
                level = z + distance
                arrived(block_of(level), q)

                @pl.when(z > 0)
                def _():
                    to_below(level, q).start()

                across(level, q, lambda copy: copy.start())

        if distance == 1:
            loads[0].wait()
            take(0)

    to_near().start()
    for order in range(1, depth):
        take(order)

    mine = pl.ds(pl.multiple_of(core * half, 16), half)
    theirs = pl.ds(pl.multiple_of(other * half, 16), half)
    shrunk_copy = pltpu.make_async_remote_copy(
        src_ref=shrunk_partial.at[theirs],
        dst_ref=shrunk_partner,
        send_sem=shrunk_sem.at[0],
        recv_sem=shrunk_sem.at[1],
        device_id={"tensor": other},
        device_id_type=MESH,
    )
    shrunk_copy.start()
    for load in loads[1:]:
        load.wait()

    def slot_copy(step):
        target = lax.rem(me + step, pool)
        return pltpu.make_async_remote_copy(
            src_ref=slot_own,
            dst_ref=slot_parts.at[step],
            send_sem=slot_send.at[step],
            recv_sem=slot_recv.at[step],
            device_id={"pool": target},
            device_id_type=MESH,
        )

    def share_shrunk():
        shrunk_copy.wait_recv()
        mask = jnp.sum(
            jnp.where(
                iota((half, LANES), 1) == me, rows_in[mine, width:].astype(jnp.float32), 0.0
            ),
            axis=1,
            keepdims=True,
        )
        total = (shrunk_partial[mine, :] + shrunk_partner[...]).astype(jnp.bfloat16)
        slot_own[...] = jnp.where(mask > 0.5, total.astype(jnp.float32), 0.0).astype(
            jnp.bfloat16
        )
        for step in range(1, pool):
            slot_copy(step).start()

    def spread_shrunk():
        total = slot_own[...].astype(jnp.float32)
        for step in range(1, pool):
            slot_copy(step).wait_recv()
            total = total + slot_parts[step].astype(jnp.float32)
        shrunk = total.astype(jnp.bfloat16)
        spread = jnp.where(
            iota((LANES, stacked), 1) // rank == iota((LANES, stacked), 0), 1.0, 0.0
        ).astype(jnp.bfloat16)
        hot_in = jnp.dot(rows_in[mine, width:], spread, preferred_element_type=jnp.float32)
        for offset, ref in ((0, gate_in), (rank, up_in)):
            repeat = jnp.where(
                iota((rank2, stacked), 1) % rank + offset == iota((rank2, stacked), 0), 1.0, 0.0
            ).astype(jnp.bfloat16)
            value = jnp.dot(shrunk, repeat, preferred_element_type=jnp.float32)
            ref[...] = (value * hot_in).astype(jnp.bfloat16)

    def partial_copy(c):
        return pltpu.make_async_remote_copy(
            src_ref=partial.at[c, :, theirs, :],
            dst_ref=partner_partial.at[c],
            send_sem=partial_send.at[c],
            recv_sem=partial_recv.at[c],
            device_id={"tensor": other},
            device_id_type=MESH,
        )

    def act_copy(c, j):
        target = core * half_pool + j
        return pltpu.make_async_remote_copy(
            src_ref=acted.at[c, j],
            dst_ref=land.at[c, me],
            send_sem=act_send.at[c, j],
            recv_sem=act_recv.at[c, me],
            device_id={"pool": target},
            device_id_type=MESH,
        )

    def columns_of(c):
        return pl.ds(pl.multiple_of(c * BLOCK, BLOCK), BLOCK)

    def project(c):
        columns = columns_of(c)
        for k, weight in enumerate((gate_w, up_w)):
            partial[c, k] = jnp.dot(
                rows_in[:, :width], weight[:, columns], preferred_element_type=jnp.float32
            )
        partial_copy(c).start()

    def activate(c):
        columns = columns_of(c)
        partial_copy(c).wait_recv()
        pre = []
        for k, (left, expander) in enumerate(((gate_in, gate_expander), (up_in, up_expander))):
            change = jnp.dot(
                left[...], expander[:, columns], preferred_element_type=jnp.float32
            )
            pre.append(
                partial[c, k, mine, :] + partner_partial[c, k] + adapter_scale_factor * change
            )
        gate, up = pre
        value = gate / (1.0 + jnp.exp(-gate)) * up
        value = value.reshape(half_pool, own_rows, BLOCK).astype(jnp.bfloat16)
        acted[c] = value
        for j in range(half_pool):
            is_own = core * half_pool + j == me

            @pl.when(jnp.logical_not(is_own))
            def _():
                act_copy(c, j).start()

            @pl.when(is_own)
            def _():
                land[c, me] = acted[c, j]

    def step_body(c, carry):
        project(c)

        @pl.when(c == 0)
        def _():
            share_shrunk()

        @pl.when(c == LAG)
        def _():
            spread_shrunk()

        @pl.when(c >= LAG)
        def _():
            activate(c - LAG)

        return carry

    lax.fori_loop(0, steps, step_body, 0)

    def late_body(c, carry):
        activate(c)
        return carry

    lax.fori_loop(steps - LAG, steps, late_body, 0)

    def share_copy(c):
        return pltpu.make_async_remote_copy(
            src_ref=land.at[c],
            dst_ref=land.at[c],
            send_sem=share_send.at[c],
            recv_sem=share_recv.at[c],
            device_id={"tensor": other},
            device_id_type=MESH,
        )

    def place(c):
        for source in range(pool):
            column = pl.multiple_of((source * steps + c) * BLOCK, BLOCK)
            out_ref[:, pl.ds(column, BLOCK)] = land[c, source]

    @pl.when(here)
    def _():
        def receive(c, carry):
            for step in range(1, pool):
                source = lax.rem(me + step, pool)
                pltpu.make_async_remote_copy(
                    src_ref=acted.at[c, 0],
                    dst_ref=land.at[c, source],
                    send_sem=act_send.at[c, 0],
                    recv_sem=act_recv.at[c, source],
                    device_id={"pool": source},
                    device_id_type=MESH,
                ).wait_recv()
            share_copy(c).start()
            place(c)
            return carry

        lax.fori_loop(0, steps, receive, 0)

    @pl.when(jnp.logical_not(here))
    def _():
        def receive(c, carry):
            share_copy(c).wait_recv()
            place(c)
            return carry

        lax.fori_loop(0, steps, receive, 0)

    def finish(c, carry):
        partial_copy(c).wait_send()
        for j in range(half_pool):

            @pl.when(core * half_pool + j != me)
            def _():
                act_copy(c, j).wait_send()

        @pl.when(here)
        def _():
            share_copy(c).wait_send()

        return carry

    lax.fori_loop(0, steps, finish, 0)
    shrunk_copy.wait_send()
    for step in range(1, pool):
        slot_copy(step).wait_send()
    for level in range(depth):
        for q in range(PIECES):
            across(level, q, lambda copy: copy.wait_send())

            @pl.when(jnp.logical_and(level <= z, z < depth - 1))
            def _():
                to_above(level, q).wait_send()

            @pl.when(jnp.logical_and(level >= z, z > 0))
            def _():
                to_below(level, q).wait_send()

    to_near().wait_send()


def fused_body(
    pool,
    hidden,
    adapter_ids,
    page_table,
    gate_weight,
    up_weight,
    shrink,
    gate_expander_matrices,
    up_expander_matrices,
):
    own_rows, width = hidden.shape
    columns = gate_weight.shape[1]
    rank2 = shrink.shape[2]
    steps = columns // BLOCK
    rows = pool * own_rows
    half = rows // 2
    half_pool = pool // 2
    stacked = gate_expander_matrices.shape[0] * gate_expander_matrices.shape[1]
    bf16, f32 = jnp.bfloat16, jnp.float32
    dma = pltpu.SemaphoreType.DMA
    vmem = pl.BlockSpec(memory_space=pltpu.VMEM)
    anywhere = pl.BlockSpec(memory_space=pl.ANY)
    result = pl.pallas_call(
        functools.partial(fused_kernel, pool),
        out_shape=jax.ShapeDtypeStruct((own_rows, pool * columns), bf16),
        in_specs=[vmem, pl.BlockSpec(memory_space=pltpu.SMEM), vmem] + [anywhere] * 5,
        out_specs=vmem,
        scratch_shapes=[
            pltpu.VMEM((pool, own_rows, width + LANES), bf16),
            pltpu.VMEM((rows, width + LANES), bf16),
            pltpu.VMEM((width, columns), bf16),
            pltpu.VMEM((width, columns), bf16),
            pltpu.VMEM((rank2, width), bf16),
            pltpu.VMEM((stacked, columns), bf16),
            pltpu.VMEM((stacked, columns), bf16),
            pltpu.VMEM((steps, 2, rows, BLOCK), f32),
            pltpu.VMEM((steps, 2, half, BLOCK), f32),
            pltpu.VMEM((rows, rank2), f32),
            pltpu.VMEM((half, rank2), f32),
            pltpu.VMEM((half, rank2), bf16),
            pltpu.VMEM((pool, half, rank2), bf16),
            pltpu.VMEM((half, stacked), bf16),
            pltpu.VMEM((half, stacked), bf16),
            pltpu.VMEM((steps, half_pool, own_rows, BLOCK), bf16),
            pltpu.VMEM((steps, pool, own_rows, BLOCK), bf16),
            dma((5,)),
            dma((4, PIECES, pool)),
            dma((PIECES, pool)),
            dma((2,)),
            dma((pool,)),
            dma((pool,)),
            dma((steps,)),
            dma((steps,)),
            dma((steps, half_pool)),
            dma((steps, pool)),
            dma((steps,)),
            dma((steps,)),
        ],
        compiler_params=pltpu.CompilerParams(
            collective_id=0, has_side_effects=True, vmem_limit_bytes=56 * 1024 * 1024
        ),
        cost_estimate=pl.CostEstimate(
            flops=4 * rows * width * columns,
            bytes_accessed=4 * width * columns,
            transcendentals=half * columns,
        ),
    )(
        adapter_ids.reshape(1, own_rows),
        page_table,
        hidden,
        gate_weight,
        up_weight,
        shrink.reshape(width, rank2).T,
        gate_expander_matrices.reshape(stacked, columns),
        up_expander_matrices.reshape(stacked, columns),
    )
    return result


def expansion_products(shrunk_part, hot_part, gate_expander_matrices, up_expander_matrices):
    rank = gate_expander_matrices.shape[1]
    number = hot_part.shape[0]
    width = gate_expander_matrices.shape[2]
    gate_in = (hot_part[:, :, None] * shrunk_part[:, None, :rank]).reshape(number, -1)
    up_in = (hot_part[:, :, None] * shrunk_part[:, None, rank:]).reshape(number, -1)
    gate_adapter_change = jnp.dot(
        gate_in, gate_expander_matrices.reshape(-1, width), preferred_element_type=jnp.float32
    )
    up_adapter_change = jnp.dot(
        up_in, up_expander_matrices.reshape(-1, width), preferred_element_type=jnp.float32
    )
    return jnp.concatenate([gate_adapter_change, up_adapter_change], axis=1)


def body(
    hidden,
    adapter_ids,
    page_table,
    gate_weight,
    up_weight,
    shrink,
    gate_expander_matrices,
    up_expander_matrices,
):
    adapters = page_table.shape[0]
    columns = gate_weight.shape[1]
    table = jnp.arange(adapters, dtype=jnp.int32)
    id_hot = adapter_ids == table[None, :]
    slot = jnp.sum(jnp.where(id_hot, page_table[None, :], 0), axis=1)
    slot_hot = (slot[:, None] == table[None, :]).astype(jnp.bfloat16)
    hot_piece = slot_hot.astype(jnp.float32)
    per_slot = jnp.einsum(
        "rd,sdk->rsk",
        hidden,
        lax.all_gather(shrink, "pool", axis=0, tiled=True),
        preferred_element_type=jnp.float32,
    )
    partial_value = jnp.einsum("rsk,rs->rk", per_slot, hot_piece, precision=lax.Precision.HIGHEST)
    shrunk = lax.psum(partial_value, "tensor").astype(jnp.bfloat16)
    piece = lax.all_gather(hidden, "pool", axis=0, tiled=True)
    gate_part = jnp.dot(piece, gate_weight, preferred_element_type=jnp.float32)
    up_part = jnp.dot(piece, up_weight, preferred_element_type=jnp.float32)
    base_part = jnp.concatenate([gate_part, up_part], axis=1)
    reduced_rows_gathered = lax.all_gather(shrunk, "pool", axis=0, tiled=True)
    slot_all = lax.all_gather(slot, "pool", axis=0, tiled=True)
    active_rows_gathered = (slot_all[:, None] == table[None, :]).astype(jnp.bfloat16)
    combined_sum = lax.psum(base_part, "tensor")
    combined_sum = combined_sum + adapter_scale_factor * expansion_products(
        reduced_rows_gathered, active_rows_gathered, gate_expander_matrices, up_expander_matrices
    )
    gate_preactivation = combined_sum[:, :columns]
    up_preactivation = combined_sum[:, columns:]
    activated = (jax.nn.silu(gate_preactivation) * up_preactivation).astype(jnp.bfloat16)
    return lax.all_to_all(activated, "pool", split_axis=0, concat_axis=1, tiled=True)


def chosen_body(pool, *args):
    hidden, _, page_table, gate_weight, _, shrink = args[:6]
    fits = (
        pool % 4 == 0
        and page_table.shape[0] == pool
        and shrink.shape[0] == 1
        and pool <= LANES
        and gate_weight.shape[1] % BLOCK == 0
        and gate_weight.shape[1] // BLOCK > LAG
        and hidden.shape[0] % 8 == 0
        and (hidden.shape[1] + LANES) % (PIECES * LANES) == 0
    )
    return fused_body(pool, *args) if fits else body(*args)


def solution(mesh):
    in_specs = (
        P(("groups", "pool"), "tensor"),
        P(("groups", "pool"), None),
        P(),
        P("tensor", "pool"),
        P("tensor", "pool"),
        P("pool", "tensor", None),
        P(None, None, "pool"),
        P(None, None, "pool"),
    )
    out_specs = P(("groups", "pool"), None)
    return jax.shard_map(
        functools.partial(chosen_body, mesh.shape["pool"]),
        mesh=mesh,
        in_specs=in_specs,
        out_specs=out_specs,
        check_vma=False,
    )
```
